32 devices in a mesh: rows: 8 (over z, y), feat: 4 (over x, core).
Axes of the slice: x: 2, y: 2, z: 4, core: 2. Of those that a mesh axis runs over, the one named last changes fastest.
Arguments:
- bin_codes: int32 [32768, 2048], P('rows', 'feat'), may hold values from 0 to 255
- gradient: bfloat16 [32768], P('rows'), may hold values from -6 to 6
- hessian: bfloat16 [32768], P('rows'), may hold values from 0.049804688 to 1
- leaf_of_block: int32 [256], P('rows'), may hold values from 0 to 1
- block_rows: int32 [256], P('rows'), may hold values from 32 to 128, as said below
Outputs:
- split_gain: float32 [2, 2048, 256], P(None, ('feat', 'rows'))
- best_gain: float32 [2], replicated
The draws below stay inside these ranges and needn't reach their ends.
Inputs may be any that keep to these rules, and one draw needn't show every extreme that they name: `block_rows`: the live rows are the first ones of their block; some block is full in every draw.
All inputs are finite; a program needn't handle non-finite values.
Results may differ from the reference program's by a relative error of at most 0.0003.
Values sent between devices are 32-bit elements; how exact they have to be, the bound alone decides.
No kernel may reach another device: no remote copies, remote signals or barrier semaphores. Data moves between devices by JAX's collectives and lax.ppermute only.
A program may use at most 64 MiB of HBM per device.

```python
import math
import jax
import jax.numpy as jnp
import numpy as np
from jax import lax

FEATURES = 2048
BINS = 256
LEAVES = 2
BLOCK = 128
MIN_CHILD = 20
ROWS = 32768
BLOCKS = 256


def draw_block_rows(key, part):
    first_key, second_key = jax.random.split(jax.random.fold_in(key, 17))
    live_rows = jax.random.randint(first_key, (BLOCKS,), BLOCK // 4, BLOCK + 1)
    full_block = jax.random.randint(second_key, (), 0, BLOCKS)
    return jnp.where(jnp.arange(BLOCKS) == full_block, BLOCK, live_rows).astype(jnp.int32)


def place_ends(values, rng, smallest, high):
    index_at = [jax.random.randint(jax.random.fold_in(rng, axis), (), 0, length) for axis, length in enumerate(values.shape)]
    main_axis = values.shape.index(max(values.shape))
    neighbour = index_at[:main_axis] + [(index_at[main_axis] + 1) % values.shape[main_axis]] + index_at[main_axis + 1:]
    return values.at[tuple(index_at)].set(smallest).at[tuple(neighbour)].set(high)


def level_of(stream_key, dims, pieces, least, high):
    gain, own = 1.0, jax.random.fold_in(stream_key, 6)
    for axis_at, parts in pieces:
        draws = jnp.exp(jax.random.uniform(jax.random.fold_in(own, axis_at), (parts,), jnp.float32, least / len(pieces), high / len(pieces)))
        gain = gain * jnp.repeat(draws, dims[axis_at] // parts).reshape([-1 if axis == axis_at else 1 for axis in range(len(dims))])
    return gain


def rank_table(number_of, slope):
    loads = [(1 << 20) // math.isqrt(rank ** slope) + 1 for rank in range(1, number_of + 1)]
    spread = 1 + sum(loads) // (1 << 30)
    return np.cumsum(np.array([max(1, weight // spread) for weight in loads]))


def ranked_ids(rng, dims, number_of, lean):
    table = rank_table(number_of, lean)
    pick = jax.random.randint(jax.random.fold_in(rng, 1), dims, 0, int(table[number_of - 1]))
    grade = jnp.searchsorted(jnp.asarray(table, jnp.int32), pick, side="right")
    return jax.random.permutation(jax.random.fold_in(rng, 2), number_of)[grade].astype(jnp.int32)


def centred(stream_key, extent, spread, most, shards=(), kind=jnp.bfloat16):
    values = spread * jax.random.normal(stream_key, extent, jnp.float32)
    if shards:
        values = values * level_of(stream_key, extent, shards, -0.22, 0.18)
    return jnp.clip(values, -most, most).astype(kind)


def setup_inputs(seed: int = 0) -> dict:
    splits = jax.random.split(jax.random.key(seed), 6)
    return {
        "bin_codes": place_ends(ranked_ids(splits[0], (ROWS, FEATURES), BINS, 2), jax.random.fold_in(splits[0], 3), 0, BINS - 1).astype(jnp.int32),
        "gradient": centred(splits[1], (ROWS,), 1.0, 6.0, ((0, 8),)),
        "hessian": jnp.clip(jnp.exp(math.log(1.0) - 2.9996462 * jax.random.uniform(splits[2], (ROWS,), jnp.float32) ** level_of(splits[2], (ROWS,), ((0, 8),), -0.2, 0.2)), 0.049804688, 1.0).astype(jnp.bfloat16),
        "leaf_of_block": place_ends(jax.random.randint(splits[3], (BLOCKS,), 0, LEAVES), jax.random.fold_in(splits[3], 1), 0, LEAVES - 1).astype(jnp.int32),
        "block_rows": draw_block_rows(jax.random.fold_in(splits[5], 71), 0),
    }


ridge_term = 1.0


def reference(bin_codes, gradient, hessian, leaf_of_block, block_rows):
    row_total = bin_codes.shape[0]
    feature_total = bin_codes.shape[1]
    offsets = jnp.arange(row_total, dtype=jnp.int32) % BLOCK
    live_rows = (offsets < jnp.repeat(block_rows, BLOCK)).astype(jnp.float32)
    leaf_ids = jnp.repeat(leaf_of_block, BLOCK).astype(jnp.int32)
    row_stats = jnp.stack([gradient.astype(jnp.float32), hessian.astype(jnp.float32), jnp.ones((row_total,), jnp.float32)], 1) * live_rows[:, None]

    def column_sums(column):
        return jax.ops.segment_sum(row_stats, leaf_ids * BINS + column, num_segments=LEAVES * BINS)

    histogram = lax.map(column_sums, bin_codes.T).reshape(feature_total, LEAVES, BINS, 3)
    running = jnp.cumsum(histogram, axis=2)
    totals = running[:, :, -1:, :]
    left_grad, left_hess, left_count = running[..., 0], running[..., 1], running[..., 2]
    total_grad, total_hess, total_count = totals[..., 0], totals[..., 1], totals[..., 2]
    right_grad = total_grad - left_grad
    right_hess = total_hess - left_hess
    right_count = total_count - left_count
    raw_gain = 0.5 * (left_grad ** 2 / (left_hess + ridge_term) + right_grad ** 2 / (right_hess + ridge_term) - total_grad ** 2 / (total_hess + ridge_term))
    allowed = (left_count >= MIN_CHILD) & (right_count >= MIN_CHILD)
    split_gain = jnp.transpose(jnp.where(allowed, raw_gain, 0.0), (1, 0, 2))
    best_gain = jnp.max(split_gain, axis=(1, 2))
    return split_gain, best_gain
```

```python
import functools

import jax
import jax.numpy as jnp
from jax import lax
from jax.experimental import pallas as pl
from jax.experimental.pallas import tpu as pltpu
from jax.sharding import PartitionSpec as P

BINS = 256
LEAVES = 2
BLOCK = 128
MIN_CHILD = 20
RIDGE = 1.0

STATS = 3
HIGH = 8
LOW = 32
FOLD = 8
PAIR = 2 * FOLD
WIDTH = LOW * FOLD
DEPTH = STATS * HIGH * FOLD
BIG = 1024
SMALL = 256
SPAN = 512
WAYS = 4

BF = jnp.bfloat16
F32 = jnp.float32
VMEM_BYTES = 56 << 20


def nt(a, b):
    return lax.dot_general(a, b, (((1,), (1,)), ((), ())), preferred_element_type=F32)


def exact(a, b):
    return lax.dot_general(
        a, b, (((1,), (0,)), ((), ())), precision=lax.Precision.HIGHEST, preferred_element_type=F32
    )


def live_up(count):
    return (count + 15) // 16 * 16


def pack_kernel(
    steps, blocks, pos_ref, leaf_ref, rows_ref, codes_ref, stats_ref, table_ref, weight_ref, info_ref, held, rows_held, offset
):
    step = pl.program_id(0)
    per_step = SPAN // BLOCK

    @pl.when(step == 0)
    def _():
        def count(k, ends):
            room = live_up(rows_ref[k])
            second = leaf_ref[k]
            return ends[0] + room * (1 - second), ends[1] + room * second

        first, second = lax.fori_loop(0, blocks, count, (0, 0))
        start = (first + SMALL - 1) // SMALL * SMALL + BLOCK

        def place(k, ends):
            room = live_up(rows_ref[k])
            leaf = leaf_ref[k]
            offset[k] = jnp.where(leaf == 0, ends[0], ends[1])
            return ends[0] + room * (1 - leaf), ends[1] + room * leaf

        lax.fori_loop(0, blocks, place, (0, start))
        for leaf, total in ((0, first), (1, second)):
            tiles = (total + SMALL - 1) // SMALL
            info_ref[2 * leaf] = tiles // (BIG // SMALL)
            info_ref[2 * leaf + 1] = tiles % (BIG // SMALL)
        info_ref[4] = start
        info_ref[5] = pos_ref[0]
        info_ref[6] = start + (second + SMALL - 1) // SMALL * SMALL
        info_ref[7] = 0
        rows_held[...] = jnp.zeros_like(rows_held)

    @pl.when(step < steps)
    def _():
        lane = lax.broadcasted_iota(jnp.int32, (8, BLOCK), 1)
        row = lax.broadcasted_iota(jnp.int32, (8, BLOCK), 0)
        for i in range(per_step):
            k = step * per_step + i
            at = pl.multiple_of(offset[k], 16)
            held[pl.ds(at, BLOCK), :] = codes_ref[i * BLOCK : (i + 1) * BLOCK, :].astype(F32).astype(BF)
            grad = jnp.broadcast_to(stats_ref[0, pl.ds(k, 1), :], (8, BLOCK))
            hess = jnp.broadcast_to(stats_ref[1, pl.ds(k, 1), :], (8, BLOCK))
            value = jnp.where(row == 0, grad, jnp.where(row == 1, hess, jnp.where(row == 2, 1.0, 0.0)))
            value = jnp.where(lane < rows_ref[k], value, 0.0)
            shift = lax.rem(at, BLOCK)
            tile = pl.multiple_of(at - shift, BLOCK)
            turned = pltpu.roll(value, shift, 1)
            here = rows_held[:, pl.ds(tile, BLOCK)]
            rows_held[:, pl.ds(tile, BLOCK)] = jnp.where(lane < shift, here, turned)
            rows_held[:, pl.ds(pl.multiple_of(tile + BLOCK, BLOCK), BLOCK)] = jnp.where(lane < shift, turned, 0.0)

    @pl.when(step >= steps)
    def _():
        at = pl.multiple_of((step - steps) * SPAN, SPAN)

        @pl.when(at < info_ref[6])
        def _():
            size = 256
            eye = (
                lax.broadcasted_iota(jnp.int32, (size, size), 0) == lax.broadcasted_iota(jnp.int32, (size, size), 1)
            ).astype(F32).astype(BF)
            for f in range(0, table_ref.shape[0], size):
                table_ref[f : f + size, :] = nt(eye, held[pl.ds(at, SPAN), f : f + size]).astype(BF)
            for s in range(STATS):
                weight_ref[s] = jnp.broadcast_to(rows_held[s : s + 1, pl.ds(at, SPAN)], (16, SPAN)).astype(BF)


def pack(pos, leaf_of_block, block_rows, codes, stats, room):
    row_total, feat_local = codes.shape
    blocks = row_total // BLOCK
    steps = row_total // SPAN
    return pl.pallas_call(
        functools.partial(pack_kernel, steps, blocks),
        grid_spec=pltpu.PrefetchScalarGridSpec(
            num_scalar_prefetch=3,
            grid=(steps + room // SPAN,),
            in_specs=[
                pl.BlockSpec((SPAN, feat_local), lambda i, *_: (jnp.minimum(i, steps - 1), 0)),
                pl.BlockSpec((2, blocks, BLOCK), lambda i, *_: (0, 0, 0)),
            ],
            out_specs=[
                pl.BlockSpec((feat_local, SPAN), lambda i, *_: (0, jnp.maximum(i - steps, 0))),
                pl.BlockSpec((STATS, 16, SPAN), lambda i, *_: (0, 0, jnp.maximum(i - steps, 0))),
                pl.BlockSpec(memory_space=pltpu.SMEM),
            ],
            scratch_shapes=[
                pltpu.VMEM((room, feat_local), BF),
                pltpu.VMEM((8, room), F32),
                pltpu.SMEM((blocks,), jnp.int32),
            ],
        ),
        out_shape=[
            jax.ShapeDtypeStruct((feat_local, room), BF),
            jax.ShapeDtypeStruct((STATS, 16, room), BF),
            jax.ShapeDtypeStruct((8,), jnp.int32),
        ],
        compiler_params=pltpu.CompilerParams(vmem_limit_bytes=VMEM_BYTES),
        cost_estimate=pl.CostEstimate(flops=4 << 30, bytes_accessed=16 << 20, transcendentals=0),
    )(pos, leaf_of_block, block_rows, codes, stats)


def histogram_kernel(add, *refs):
    info_ref = refs[0]
    tables = refs[1 : 1 + WAYS]
    weight_ref = refs[1 + WAYS]
    if add:
        recv_ref = refs[2 + WAYS]
        outs, total = refs[3 + WAYS : 3 + 2 * WAYS], refs[3 + 2 * WAYS]
    else:
        outs, total = refs[2 + WAYS : 3 + WAYS], refs[3 + WAYS]
    folds = 2 * WAYS
    lane = lax.broadcasted_iota(jnp.int32, (FOLD, WIDTH), 1)
    skew = (lax.broadcasted_iota(jnp.int32, (FOLD, WIDTH), 0) - lane) & (FOLD - 1)

    def product(at, size):
        half = (lax.broadcasted_iota(jnp.int32, (16, size), 0) // FOLD).astype(F32).astype(BF)
        one, zero = jnp.ones((16, size), BF), jnp.zeros((16, size), BF)
        weights = [weight_ref[s, :, pl.ds(at, size)] for s in range(STATS)]
        for way in range(WAYS):
            both = tables[way][:, pl.ds(at, size)].astype(F32)
            for i in range(2):
                code = both[i * FOLD : (i + 1) * FOLD]
                high = jnp.floor(code * (1.0 / LOW))
                low = code - high * LOW
                high = jnp.concatenate([high, high], 0).astype(BF) - half
                low = jnp.concatenate([low, low], 0).astype(BF) - half
                picks = jnp.concatenate([jnp.where(low == BF(2 * q), one, zero) for q in range(LOW // 2)], 0)
                masks = [high == BF(2 * q) for q in range(HIGH // 2)]
                terms = jnp.concatenate([jnp.where(m, w, zero) for w in weights for m in masks], 0)
                total[2 * way + i] += nt(terms, picks)

    for leaf in range(LEAVES):
        total[...] = jnp.zeros_like(total)
        start = info_ref[4] if leaf else 0
        big, small = info_ref[2 * leaf], info_ref[2 * leaf + 1]

        @pl.loop(0, big)
        def _(k):
            product(pl.multiple_of(start + k * BIG, BLOCK), BIG)

        @pl.loop(0, small)
        def _(k):
            product(pl.multiple_of(start + big * BIG + k * SMALL, BLOCK), SMALL)

        for way in range(WAYS):
            for i in range(2):
                for s in range(STATS):
                    base = s * HIGH * FOLD
                    value = total[2 * way + i, base : base + FOLD]
                    for h in range(1, HIGH):
                        piece = total[2 * way + i, base + h * FOLD : base + (h + 1) * FOLD]
                        value = jnp.where(skew == h, pltpu.roll(piece, h, 0), value)
                    if add:
                        outs[way][i, leaf, s] = value + recv_ref[way, i, leaf, s]
                    else:
                        outs[0][way, i, leaf, s] = value


def histogram(info, table, weight, owners, chunk, ways, other, recv):
    room = table.shape[1]
    per_owner = table.shape[0] // owners // PAIR
    add = recv is not None

    def at(way):
        def index(i, info):
            pos = info[5]
            owner = ((pos // 2) ^ way) * 2 + ((pos & 1) ^ other)
            return owner * per_owner + chunk, 0

        return index

    block = (2, LEAVES, STATS, FOLD, WIDTH)
    if add:
        out_shape = [jax.ShapeDtypeStruct(block, F32)] * WAYS
        out_specs = [pl.BlockSpec(block, lambda i, info: (0,) * 5)] * WAYS
    else:
        out_shape = [jax.ShapeDtypeStruct((WAYS,) + block, F32)]
        out_specs = [pl.BlockSpec((WAYS,) + block, lambda i, info: (0,) * 6)]
    return pl.pallas_call(
        functools.partial(histogram_kernel, add),
        grid_spec=pltpu.PrefetchScalarGridSpec(
            num_scalar_prefetch=1,
            grid=(1,),
            in_specs=[pl.BlockSpec((PAIR, room), at(way)) for way in ways]
            + [pl.BlockSpec((STATS, 16, room), lambda i, info: (0, 0, 0))]
            + ([pl.BlockSpec((WAYS,) + block, lambda i, info: (0,) * 6)] if add else []),
            out_specs=out_specs,
            scratch_shapes=[pltpu.VMEM((2 * WAYS, DEPTH, WIDTH), F32)],
        ),
        out_shape=out_shape,
        compiler_params=pltpu.CompilerParams(vmem_limit_bytes=VMEM_BYTES),
        cost_estimate=pl.CostEstimate(flops=6 << 30, bytes_accessed=4 << 20, transcendentals=0),
    )(info, *([table] * WAYS), weight, *([recv] if add else []))


def gain_kernel(parts, *refs):
    own = refs[:parts]
    best_ref = refs[parts + 1]
    gain_ref, top_ref = refs[parts + 2], refs[parts + 3]
    lane = lax.broadcasted_iota(jnp.int32, (FOLD, WIDTH), 1)
    row = lax.broadcasted_iota(jnp.int32, (FOLD, WIDTH), 0)
    rows = lax.broadcasted_iota(jnp.int32, (WIDTH, WIDTH), 0)
    cols = lax.broadcasted_iota(jnp.int32, (WIDTH, WIDTH), 1)
    same = (rows % FOLD) == (cols % FOLD)
    upto = (same & (rows // FOLD <= cols // FOLD)).astype(F32)
    same = same.astype(F32)
    order = ((rows % FOLD == cols // LOW) & (rows // FOLD == cols % LOW)).astype(F32)
    pieces = []
    for i in range(2):
        for leaf in range(LEAVES):
            for s in range(STATS):
                x = own[0][i, leaf, s]
                for p in range(1, parts):
                    x = x + own[p][i, leaf, s]
                for bit in (1, 2, 4):
                    x = jnp.where((lane & bit) != 0, pltpu.roll(x, FOLD - bit, 0), x)
                pieces.append(x)
    stacked = jnp.concatenate(pieces, 0)
    inner = exact(stacked, upto)
    whole = exact(stacked, same)
    gains = []
    for i in range(2):
        for leaf in range(LEAVES):
            left, total = [], []
            for s in range(STATS):
                at = ((i * LEAVES + leaf) * STATS + s) * FOLD
                sums = whole[at : at + FOLD]
                run = sums
                for step in (1, 2, 4):
                    run = run + jnp.where(row >= step, pltpu.roll(run, step, 0), 0.0)
                before = jnp.where(row >= 1, pltpu.roll(run, 1, 0), 0.0)
                left.append(inner[at : at + FOLD] + before)
                total.append(jnp.broadcast_to(run[FOLD - 1 : FOLD], (FOLD, WIDTH)))
            right = [t - a for t, a in zip(total, left)]
            raw = 0.5 * (
                left[0] * left[0] / (left[1] + RIDGE)
                + right[0] * right[0] / (right[1] + RIDGE)
                - total[0] * total[0] / (total[1] + RIDGE)
            )
            gains.append(jnp.where((left[2] >= MIN_CHILD) & (right[2] >= MIN_CHILD), raw, 0.0))
    turned = exact(jnp.concatenate(gains, 0), order)
    for i in range(2):
        for leaf in range(LEAVES):
            at = (i * LEAVES + leaf) * FOLD
            z = turned[at : at + FOLD]
            out = jnp.where(((row - lane // LOW) & (FOLD - 1)) == 0, z, 0.0)
            for d in range(1, FOLD):
                part = jnp.where(((row - lane // LOW) & (FOLD - 1)) == d, z, 0.0)
                out = out + pltpu.roll(pltpu.roll(part, FOLD - d, 0), LOW * d, 1)
            gain_ref[leaf, i * FOLD : (i + 1) * FOLD, :] = out
    tops = [
        jnp.max(jnp.maximum(gains[leaf], gains[LEAVES + leaf]), axis=(0, 1), keepdims=True) for leaf in range(LEAVES)
    ]
    at = lax.broadcasted_iota(jnp.int32, top_ref.shape, 1)
    top_ref[...] = jnp.maximum(best_ref[...], jnp.where(at == 0, tops[0], tops[1]))


def gain(parts, chunk, split_gain, best):
    block = (2, LEAVES, STATS, FOLD, WIDTH)
    count = len(parts)
    return pl.pallas_call(
        functools.partial(gain_kernel, count),
        grid=(1,),
        in_specs=[pl.BlockSpec(block, lambda i: (0,) * 5)] * count
        + [pl.BlockSpec(memory_space=pl.ANY), pl.BlockSpec(best.shape, lambda i: (0, 0))],
        out_specs=[
            pl.BlockSpec((LEAVES, PAIR, BINS), lambda i: (0, chunk, 0)),
            pl.BlockSpec(best.shape, lambda i: (0, 0)),
        ],
        out_shape=[
            jax.ShapeDtypeStruct(split_gain.shape, F32),
            jax.ShapeDtypeStruct(best.shape, F32),
        ],
        input_output_aliases={count: 0, count + 1: 1},
        compiler_params=pltpu.CompilerParams(vmem_limit_bytes=VMEM_BYTES),
    )(*parts, split_gain, best)


def local(owners, devices, bin_codes, gradient, hessian, leaf_of_block, block_rows):
    row_total, feat_local = bin_codes.shape
    blocks = row_total // BLOCK
    pos = lax.axis_index("rows").astype(jnp.int32)[None]
    stats = jnp.stack([gradient.reshape(blocks, BLOCK), hessian.reshape(blocks, BLOCK)]).astype(F32)
    room = -(-(row_total + 2 * SMALL + BLOCK) // SPAN) * SPAN
    table, weight, info = pack(pos, leaf_of_block, block_rows, bin_codes, stats, room)
    chunks = feat_local // owners // PAIR
    sides = owners // 2
    swap = [(i, i ^ 1) for i in range(owners)]
    split_gain = jnp.zeros((LEAVES, feat_local // owners, BINS), F32)
    best = jnp.full((devices, 128), -jnp.inf, F32)

    def to_partner(chunk):
        return [
            lax.ppermute(
                histogram(info, table, weight, owners, chunk, range(base, base + WAYS), 1, None)[0], "rows", swap
            )
            for base in range(0, sides, WAYS)
        ]

    received = {0: to_partner(0)}
    for chunk in range(chunks):
        if chunk + 1 < chunks:
            received[chunk + 1] = to_partner(chunk + 1)
        mine = []
        for base in range(0, sides, WAYS):
            mine += histogram(
                info, table, weight, owners, chunk, range(base, base + WAYS), 0, received[chunk][base // WAYS]
            )
        parts = [mine[0]]
        for way in range(1, sides):
            parts.append(lax.ppermute(mine[way], "rows", [(i, i ^ (2 * way)) for i in range(owners)]))
        split_gain, best = gain(parts, chunk, split_gain, best)
    best = lax.all_to_all(best, ("rows", "feat"), 0, 0, tiled=True)
    return split_gain, jnp.max(best, axis=0)[:LEAVES]


def solution(mesh):
    return jax.shard_map(
        functools.partial(local, mesh.shape["rows"], mesh.size),
        mesh=mesh,
        in_specs=(P("rows", "feat"), P("rows"), P("rows"), P("rows"), P("rows")),
        out_specs=(P(None, ("feat", "rows"), None), P()),
        check_vma=False,
    )
```

```python
import functools

import jax
import jax.numpy as jnp
from jax import lax
from jax.experimental import pallas as pl
from jax.experimental.pallas import tpu as pltpu
from jax.sharding import PartitionSpec as P

BINS = 256
LEAVES = 2
BLOCK = 128
MIN_CHILD = 20
RIDGE = 1.0

STATS = 3
HIGH = 8
LOW = 32
FOLD = 8
PAIR = 2 * FOLD
WIDTH = LOW * FOLD
ROWS = HIGH * FOLD
DEPTH = STATS * ROWS
TILE = 256
BIG = 4 * TILE
SPAN = 512
SIDE = 2
BLOCK_SHAPE = (2, LEAVES, STATS, FOLD, WIDTH)

BF = jnp.bfloat16
F32 = jnp.float32
VMEM_BYTES = 32 << 20


def nt(a, b):
    return lax.dot_general(a, b, (((1,), (1,)), ((), ())), preferred_element_type=F32)


def live_up(count):
    return (count + 15) // 16 * 16


def tiles_of(total):
    return (total + TILE - 1) // TILE


def pack_kernel(
    blocks,
    pos_ref, leaf_ref, rows_ref, codes_ref, stats_ref,
    table_ref, weight_ref, info_ref,
    arrived, held, turned, rows_held, offset, in_sem, out_sem,
):
    steps = blocks * BLOCK // SPAN
    per_step = SPAN // BLOCK
    feats = held.shape[1]

    def fetch(i):
        return pltpu.make_async_copy(
            codes_ref.at[pl.ds(pl.multiple_of(i * SPAN, SPAN), SPAN), :], arrived.at[i], in_sem.at[i]
        )

    for i in range(steps):
        fetch(i).start()

    def count(k, ends):
        room, leaf = live_up(rows_ref[k]), leaf_ref[k]
        return ends[0] + room * (1 - leaf), ends[1] + room * leaf

    first, second = lax.fori_loop(0, blocks, count, (0, 0), unroll=4)
    start = tiles_of(first) * TILE + BLOCK

    def place(k, ends):
        leaf = leaf_ref[k]
        offset[k] = jnp.where(leaf == 0, ends[0], ends[1])
        return count(k, ends)

    lax.fori_loop(0, blocks, place, (0, start), unroll=4)
    info_ref[0] = tiles_of(first)
    info_ref[1] = tiles_of(second)
    info_ref[2] = start
    info_ref[3] = pos_ref[0]

    rows_held[...] = jnp.zeros_like(rows_held)
    grads, hessians = stats_ref[0], stats_ref[1]
    lane = lax.broadcasted_iota(jnp.int32, (8, BLOCK), 1)
    row = lax.broadcasted_iota(jnp.int32, (8, BLOCK), 0)
    rolled = []
    for k in range(blocks):
        grad = jnp.broadcast_to(grads[k : k + 1], (8, BLOCK))
        hess = jnp.broadcast_to(hessians[k : k + 1], (8, BLOCK))
        value = jnp.where(row == 0, grad, jnp.where(row == 1, hess, jnp.where(row == 2, 1.0, 0.0)))
        value = jnp.where(lane < rows_ref[k], value, 0.0)
        rolled.append(pltpu.roll(value, lax.rem(offset[k], BLOCK), 1))
    for k in range(blocks):
        at = offset[k]
        shift = lax.rem(at, BLOCK)
        tile = pl.multiple_of(at - shift, BLOCK)
        here = rows_held[:, pl.ds(tile, BLOCK)]
        rows_held[:, pl.ds(tile, BLOCK)] = jnp.where(lane < shift, here, rolled[k])
        after = pl.ds(pl.multiple_of(tile + BLOCK, BLOCK), BLOCK)
        rows_held[:, after] = jnp.where(lane < shift, rolled[k], 0.0)

    @pl.loop(0, steps)
    def _(i):
        fetch(i).wait()
        for j in range(per_step):
            at = pl.multiple_of(offset[i * per_step + j], 16)
            held[pl.ds(at, BLOCK), :] = arrived[i, j * BLOCK : (j + 1) * BLOCK, :].astype(F32).astype(BF)

    size = 256
    eye = (
        lax.broadcasted_iota(jnp.int32, (size, size), 0) == lax.broadcasted_iota(jnp.int32, (size, size), 1)
    ).astype(F32).astype(BF)

    def span(i):
        return pl.ds(pl.multiple_of(i * SPAN, SPAN), SPAN)

    def store(i):
        return pltpu.make_async_copy(turned.at[:, span(i)], table_ref.at[:, span(i)], out_sem)

    used = (start + tiles_of(second) * TILE + SPAN - 1) // SPAN

    @pl.loop(0, used)
    def _(i):
        for f in range(0, feats, size):
            turned[f : f + size, span(i)] = nt(eye, held[span(i), f : f + size]).astype(BF)
        store(i).start()
        for s in range(STATS):
            weight_ref[s, :, span(i)] = jnp.broadcast_to(rows_held[s : s + 1, span(i)], (16, SPAN)).astype(BF)

    @pl.loop(0, used)
    def _(i):
        store(i).wait()


def pack(pos, leaf_of_block, block_rows, codes, stats, room):
    row_total, feat_local = codes.shape
    blocks = row_total // BLOCK
    steps = row_total // SPAN
    smem, whole = pl.BlockSpec(memory_space=pltpu.SMEM), pl.BlockSpec(memory_space=pltpu.VMEM)
    return pl.pallas_call(
        functools.partial(pack_kernel, blocks),
        in_specs=[smem, smem, smem, pl.BlockSpec(memory_space=pl.ANY), whole],
        out_specs=[pl.BlockSpec(memory_space=pl.ANY), whole, smem],
        scratch_shapes=[
            pltpu.VMEM((steps, SPAN, feat_local), jnp.int32),
            pltpu.VMEM((room, feat_local), BF),
            pltpu.VMEM((feat_local, room), BF),
            pltpu.VMEM((8, room), F32),
            pltpu.SMEM((blocks,), jnp.int32),
            pltpu.SemaphoreType.DMA((steps,)),
            pltpu.SemaphoreType.DMA,
        ],
        out_shape=[
            jax.ShapeDtypeStruct((feat_local, room), BF),
            jax.ShapeDtypeStruct((STATS, 16, room), BF),
            jax.ShapeDtypeStruct((8,), jnp.int32),
        ],
        compiler_params=pltpu.CompilerParams(vmem_limit_bytes=VMEM_BYTES),
        cost_estimate=pl.CostEstimate(flops=4 << 30, bytes_accessed=16 << 20, transcendentals=0),
    )(pos, leaf_of_block, block_rows, codes, stats)


def histogram_kernel(ways, keeps, add, *refs):
    info_ref, tables, weight_ref = refs[0], refs[1 : 1 + ways], refs[1 + ways]
    refs = refs[2 + ways :]
    recv_ref = None
    if add:
        recv_ref, refs = refs[0], refs[1:]
    outs, total = refs[:-1], refs[-1]
    lane = lax.broadcasted_iota(jnp.int32, (FOLD, WIDTH), 1)
    skew = (lax.broadcasted_iota(jnp.int32, (FOLD, WIDTH), 0) - lane) & (FOLD - 1)

    def product(at, size, fresh):
        half = (lax.broadcasted_iota(jnp.int32, (16, size), 0) >> 3).astype(F32).astype(BF)
        nth = (lax.broadcasted_iota(jnp.int32, (size, 128), 1) >> 3).astype(F32).astype(BF)
        one, zero = jnp.ones((size, 128), BF), jnp.zeros((size, 128), BF)
        none = jnp.zeros((16, size), BF)
        weights = [weight_ref[s, :, pl.ds(at, size)] for s in range(STATS)]
        for way in range(ways):
            both = tables[way][:, pl.ds(at, size)].astype(F32)
            for i in range(2):
                code = both[i * FOLD : (i + 1) * FOLD]
                high = jnp.floor(code * (1.0 / LOW))
                low = code - high * LOW
                high = jnp.concatenate([high] * 2, 0).astype(BF) - half
                masks = [high == BF(q) for q in range(0, HIGH, 2)]
                terms = jnp.concatenate([jnp.where(m, w, none) for w in weights for m in masks], 0)
                low = jnp.concatenate([jnp.concatenate([low] * 2, 0).astype(BF)] * 8, 0).T - nth
                picks = jnp.concatenate([jnp.where(low == BF(q), one, zero) for q in (0, 16)], 1)
                sums = lax.dot_general(terms, picks, (((1,), (0,)), ((), ())), preferred_element_type=F32)
                total[2 * way + i] = jnp.where(fresh, 0.0, total[2 * way + i]) + sums

    for leaf in range(LEAVES):
        start = info_ref[2] if leaf else 0
        tiles = info_ref[leaf]
        big = tiles // 4

        @pl.when(tiles == 0)
        def _():
            total[...] = jnp.zeros_like(total)

        @pl.loop(0, big)
        def _(k):
            product(pl.multiple_of(start + k * BIG, BLOCK), BIG, k == 0)

        at = start + big * BIG

        @pl.when((tiles & 2) != 0)
        def _():
            product(pl.multiple_of(at, BLOCK), 2 * TILE, tiles < 4)

        @pl.when((tiles & 1) != 0)
        def _():
            product(pl.multiple_of(at + (tiles & 2) * TILE, BLOCK), TILE, tiles == 1)

        for way in range(ways):
            out, nth = (outs[0], way) if way < keeps else (outs[1], way - keeps)
            for i in range(2):
                for s in range(STATS):
                    base = s * ROWS
                    value = total[2 * way + i, base : base + FOLD]
                    for h in range(1, HIGH):
                        piece = total[2 * way + i, base + h * FOLD : base + (h + 1) * FOLD]
                        value = jnp.where(skew == h, pltpu.roll(piece, h, 0), value)
                    out[nth, i, leaf, s] = value + recv_ref[way, i, leaf, s] if add else value


def histogram(packed, owners, chunk, keep, send, recv):
    table, weight, info = packed
    room = table.shape[1]
    per_owner = table.shape[0] // owners // PAIR
    ways = keep + send

    def at(way):
        return lambda i, info: ((info[3] ^ way) * per_owner + chunk, 0)

    def whole(shape):
        return pl.BlockSpec(shape, lambda i, info: (0,) * len(shape))

    out = [(len(side),) + BLOCK_SHAPE for side in (keep, send) if side]
    return pl.pallas_call(
        functools.partial(histogram_kernel, len(ways), len(keep), recv is not None),
        grid_spec=pltpu.PrefetchScalarGridSpec(
            num_scalar_prefetch=1,
            grid=(1,),
            in_specs=[pl.BlockSpec((PAIR, room), at(way)) for way in ways]
            + [whole(weight.shape)]
            + ([whole(recv.shape)] if recv is not None else []),
            out_specs=[whole(shape) for shape in out],
            scratch_shapes=[pltpu.VMEM((2 * len(ways), DEPTH, WIDTH), F32)],
        ),
        out_shape=[jax.ShapeDtypeStruct(shape, F32) for shape in out],
        compiler_params=pltpu.CompilerParams(vmem_limit_bytes=VMEM_BYTES),
        cost_estimate=pl.CostEstimate(flops=6 << 30, bytes_accessed=4 << 20, transcendentals=0),
    )(info, *([table] * len(ways)), weight, *([recv] if recv is not None else []))


def pick(x, chooser):
    total = 0.0
    for _ in range(3):
        part = x.astype(BF)
        total = total + lax.dot_general(part, chooser, (((1,), (0,)), ((), ())), preferred_element_type=F32)
        x = x - part.astype(F32)
    return total


def gain_kernel(chunks, *refs):
    own, others, gain_ref, top_ref = refs[:chunks], refs[chunks : 2 * chunks], refs[-2], refs[-1]
    lane = lax.broadcasted_iota(jnp.int32, (FOLD, WIDTH), 1)
    row = lax.broadcasted_iota(jnp.int32, (FOLD, WIDTH), 0)
    rows = lax.broadcasted_iota(jnp.int32, (WIDTH, WIDTH), 0)
    cols = lax.broadcasted_iota(jnp.int32, (WIDTH, WIDTH), 1)

    def chooser(mask):
        return jnp.where(mask, 1.0, 0.0).astype(BF)

    same = (rows & 7) == (cols & 7)
    upto = chooser(same & ((rows >> 3) <= (cols >> 3)))
    same = chooser(same)
    order = chooser(((rows & 7) == (cols >> 5)) & ((rows >> 3) == (cols & 31)))
    apart = (row - (lane >> 5)) & 7
    tops = [jnp.full((FOLD, WIDTH), -jnp.inf, F32)] * LEAVES
    for c in range(chunks):
        pieces = []
        for i in range(2):
            for leaf in range(LEAVES):
                for s in range(STATS):
                    x = own[c][0, i, leaf, s] + others[c][0, i, leaf, s]
                    for bit in (1, 2, 4):
                        x = jnp.where((lane & bit) != 0, pltpu.roll(x, FOLD - bit, 0), x)
                    pieces.append(x)
        stacked = jnp.concatenate(pieces, 0)
        inner = pick(stacked, upto)
        whole = pick(stacked, same)
        gains = []
        for i in range(2):
            for leaf in range(LEAVES):
                left, total = [], []
                for s in range(STATS):
                    at = ((i * LEAVES + leaf) * STATS + s) * FOLD
                    run = whole[at : at + FOLD]
                    for step in (1, 2, 4):
                        run = run + jnp.where(row >= step, pltpu.roll(run, step, 0), 0.0)
                    before = jnp.where(row >= 1, pltpu.roll(run, 1, 0), 0.0)
                    left.append(inner[at : at + FOLD] + before)
                    total.append(jnp.broadcast_to(run[FOLD - 1 : FOLD], (FOLD, WIDTH)))
                right = [t - a for t, a in zip(total, left)]
                raw = 0.5 * (
                    left[0] * left[0] / (left[1] + RIDGE)
                    + right[0] * right[0] / (right[1] + RIDGE)
                    - total[0] * total[0] / (total[1] + RIDGE)
                )
                value = jnp.where((left[2] >= MIN_CHILD) & (right[2] >= MIN_CHILD), raw, 0.0)
                gains.append(value)
                tops[leaf] = jnp.maximum(tops[leaf], value)
        z = pick(jnp.concatenate(gains, 0), order)
        for i in range(2):
            for leaf in range(LEAVES):
                at = (i * LEAVES + leaf) * FOLD
                piece = z[at : at + FOLD]
                out = jnp.where(apart == 0, piece, 0.0)
                for d in range(1, FOLD):
                    part = jnp.where(apart == d, piece, 0.0)
                    out = out + pltpu.roll(pltpu.roll(part, FOLD - d, 0), LOW * d, 1)
                gain_ref[leaf, c * PAIR + i * FOLD : c * PAIR + (i + 1) * FOLD, :] = out
    tops = [jnp.max(top, axis=(0, 1), keepdims=True) for top in tops]
    at = lax.broadcasted_iota(jnp.int32, top_ref.shape, 1)
    top_ref[...] = jnp.where(at == 0, tops[0], tops[1])


def gain(own, others, features, devices):
    whole = pl.BlockSpec(memory_space=pltpu.VMEM)
    return pl.pallas_call(
        functools.partial(gain_kernel, len(own)),
        in_specs=[whole] * (2 * len(own)),
        out_specs=[whole] * 2,
        out_shape=[
            jax.ShapeDtypeStruct((LEAVES, features, BINS), F32),
            jax.ShapeDtypeStruct((devices, 128), F32),
        ],
        compiler_params=pltpu.CompilerParams(vmem_limit_bytes=VMEM_BYTES),
    )(*own, *others)


def in_halves(ways, bits):
    if not bits:
        return ways
    return in_halves([w for w in ways if not w & bits[0]], bits[1:]) + in_halves(
        [w for w in ways if w & bits[0]], bits[1:]
    )


def local(owners, devices, bin_codes, gradient, hessian, leaf_of_block, block_rows):
    row_total, feat_local = bin_codes.shape
    blocks = row_total // BLOCK
    pos = lax.axis_index("rows").astype(jnp.int32)[None]
    stats = jnp.stack([gradient.reshape(blocks, BLOCK), hessian.reshape(blocks, BLOCK)]).astype(F32)
    room = -(-(row_total + 2 * TILE + BLOCK) // SPAN) * SPAN
    packed = pack(pos, leaf_of_block, block_rows, bin_codes, stats, room)
    chunks = feat_local // owners // PAIR
    bits = [1 << b for b in range(owners.bit_length() - 1)]
    kept = in_halves([w for w in range(owners) if not w & 3], bits[2:])
    calls = [kept[i : i + SIDE] for i in range(0, len(kept), SIDE)]

    def swap(x, bit):
        return lax.ppermute(x, "rows", [(i, i ^ bit) for i in range(owners)])

    def to_partner(chunk):
        return [
            swap(histogram(packed, owners, chunk, [w ^ 1 for w in call] + [w ^ 3 for w in call], [], None)[0], 1)
            for call in calls
        ]

    received = [to_partner(0)]
    own, others = [], []
    for chunk in range(chunks):
        if chunk + 1 < chunks:
            received.append(to_partner(chunk + 1))
        keep, send = [], []
        for call, recv in zip(calls, received[chunk]):
            a, b = histogram(packed, owners, chunk, call, [w ^ 2 for w in call], recv)
            keep.append(a)
            send.append(swap(b, 2))
        keep, other = (x[0] if len(x) == 1 else jnp.concatenate(x, 0) for x in (keep, send))
        for bit in bits[2:]:
            half = keep.shape[0] // 2
            on = keep[half:] + other[half:]
            keep, other = keep[:half] + other[:half], swap(on, bit)
        own.append(keep)
        others.append(other)
    split_gain, best = gain(own, others, feat_local // owners, devices)
    best = lax.all_to_all(best, ("rows", "feat"), 0, 0, tiled=True)
    return split_gain, jnp.max(best, axis=0)[:LEAVES]


def solution(mesh):
    return jax.shard_map(
        functools.partial(local, mesh.shape["rows"], mesh.size),
        mesh=mesh,
        in_specs=(P("rows", "feat"), P("rows"), P("rows"), P("rows"), P("rows")),
        out_specs=(P(None, ("feat", "rows"), None), P()),
        check_vma=False,
    )
```

```python
import functools

import jax
import jax.numpy as jnp
from jax import lax
from jax.experimental import pallas as pl
from jax.experimental.pallas import tpu as pltpu
from jax.sharding import PartitionSpec as P

BINS = 256
LEAVES = 2
BLOCK = 128
MIN_CHILD = 20
RIDGE = 1.0

STATS = 3
HIGH = 8
LOW = 32
FOLD = 8
PAIR = 2 * FOLD
WIDTH = LOW * FOLD
ROWS = HIGH * FOLD
DEPTH = STATS * ROWS
TILE = 256
BIG = 4 * TILE
SPAN = 512
WAYS = 4
PLAN = (
    ([(1, 1), (2, 1)], []),
    ([(3, 1), (0, 0)], [0]),
    ([(1, 0), (2, 0)], [1, 0]),
    ([(3, 0)], [2, 1]),
    ([], [3, 2, 3]),
)
SUMS = (2, LEAVES, STATS, FOLD, WIDTH)

BF = jnp.bfloat16
F32 = jnp.float32
VMEM_BYTES = 24 << 20
MOST_VMEM = 54 << 20


def nt(a, b):
    return lax.dot_general(a, b, (((1,), (1,)), ((), ())), preferred_element_type=F32)


def in_vmem(x):
    return pltpu.with_memory_space_constraint(x, pltpu.VMEM)


def live_up(count):
    return (count + 15) // 16 * 16


def tiles_of(total):
    return (total + TILE - 1) // TILE


def pack_kernel(
    blocks, first_rows,
    pos_ref, leaf_ref, rows_ref, codes_ref, grad_ref, hess_ref,
    table_ref, weight_ref, sums_ref, info_ref,
    arrived, held, rows_held, pair_held, total, offset, ends, in_sem, pair_sem,
):
    steps = blocks * BLOCK // SPAN
    per_step = SPAN // BLOCK
    feats = held.shape[1]

    def fetch(i):
        return pltpu.make_async_copy(
            codes_ref.at[pl.ds(pl.multiple_of(i * SPAN, SPAN), SPAN), :], arrived.at[i], in_sem.at[i]
        )

    pairs = [
        pltpu.make_async_copy(ref, pair_held.at[i], pair_sem.at[i]) for i, ref in enumerate((grad_ref, hess_ref))
    ]
    for copy in pairs:
        copy.start()
    for i in range(steps):
        fetch(i).start()

    def count(k, room):
        size, leaf = live_up(rows_ref[k]), leaf_ref[k]
        return room[0] + size * (1 - leaf), room[1] + size * leaf

    first, second = lax.fori_loop(0, blocks, count, (0, 0), unroll=4)
    start = tiles_of(first) * TILE + BLOCK

    def place(k, room):
        offset[k] = jnp.where(leaf_ref[k] == 0, room[0], room[1])
        room = count(k, room)
        ends[0, k], ends[1, k] = room
        return room

    lax.fori_loop(0, blocks, place, (0, start), unroll=4)
    info_ref[0] = tiles_of(first)
    info_ref[1] = tiles_of(second)
    info_ref[2] = start
    info_ref[3] = pos_ref[0]

    rows_held[...] = jnp.zeros_like(rows_held)
    for copy in pairs:
        copy.wait()
    grads, hessians = pair_held[0].astype(F32), pair_held[1].astype(F32)
    lane = lax.broadcasted_iota(jnp.int32, (8, BLOCK), 1)
    row = lax.broadcasted_iota(jnp.int32, (8, BLOCK), 0)
    rolled = []
    for k in range(blocks):
        grad = jnp.broadcast_to(grads[k : k + 1], (8, BLOCK))
        hess = jnp.broadcast_to(hessians[k : k + 1], (8, BLOCK))
        value = jnp.where(row == 0, grad, jnp.where(row == 1, hess, jnp.where(row == 2, 1.0, 0.0)))
        value = jnp.where(lane < rows_ref[k], value, 0.0)
        rolled.append(pltpu.roll(value, lax.rem(offset[k], BLOCK), 1))
    for k in range(blocks):
        at = offset[k]
        shift = lax.rem(at, BLOCK)
        tile = pl.multiple_of(at - shift, BLOCK)
        here = rows_held[:, pl.ds(tile, BLOCK)]
        rows_held[:, pl.ds(tile, BLOCK)] = jnp.where(lane < shift, here, rolled[k])
        after = pl.ds(pl.multiple_of(tile + BLOCK, BLOCK), BLOCK)
        rows_held[:, after] = jnp.where(lane < shift, rolled[k], 0.0)

    size = 256
    eye = (
        lax.broadcasted_iota(jnp.int32, (size, size), 0) == lax.broadcasted_iota(jnp.int32, (size, size), 1)
    ).astype(F32).astype(BF)

    def turn(base, tiles, done):
        @pl.loop(done, tiles)
        def _(j):
            at = pl.multiple_of(base + j * TILE, BLOCK)
            for f in range(0, feats, size):
                table_ref[f : f + size, pl.ds(at, TILE)] = nt(eye, held[pl.ds(at, TILE), f : f + size]).astype(BF)
            for s in range(STATS):
                weight_ref[s, :, pl.ds(at, TILE)] = jnp.broadcast_to(
                    rows_held[s : s + 1, pl.ds(at, TILE)], (16, TILE)
                ).astype(BF)

        return jnp.maximum(done, tiles)

    def step(i, done):
        fetch(i).wait()
        for j in range(per_step):
            at = pl.multiple_of(offset[i * per_step + j], 16)
            held[pl.ds(at, BLOCK), :] = arrived[i, j * BLOCK : (j + 1) * BLOCK, :].astype(F32).astype(BF)
        last = (i + 1) * per_step - 1
        return (
            turn(0, ends[0, last] // TILE, done[0]),
            turn(start, (ends[1, last] - start) // TILE, done[1]),
        )

    done = lax.fori_loop(0, steps, step, (0, 0))
    turn(0, tiles_of(first), done[0])
    turn(start, tiles_of(second), done[1])
    histogram_into(first_rows(info_ref), info_ref, table_ref, weight_ref, [sums_ref], total)


def pack(pos, leaf_of_block, block_rows, codes, gradient, hessian, room, first_rows):
    row_total, feat_local = codes.shape
    blocks = row_total // BLOCK
    steps = row_total // SPAN
    whole, anywhere = pl.BlockSpec(memory_space=pltpu.VMEM), pl.BlockSpec(memory_space=pl.ANY)
    return pl.pallas_call(
        functools.partial(pack_kernel, blocks, first_rows),
        grid_spec=pltpu.PrefetchScalarGridSpec(
            num_scalar_prefetch=3,
            grid=(1,),
            in_specs=[anywhere] * 3,
            out_specs=[whole, whole, whole, pl.BlockSpec(memory_space=pltpu.SMEM)],
            scratch_shapes=[
                pltpu.VMEM((steps, SPAN, feat_local), jnp.int32),
                pltpu.VMEM((room, feat_local), BF),
                pltpu.VMEM((8, room), F32),
                pltpu.VMEM((2, blocks, BLOCK), BF),
                pltpu.VMEM((2 * WAYS, DEPTH, WIDTH), F32),
                pltpu.SMEM((blocks,), jnp.int32),
                pltpu.SMEM((2, blocks), jnp.int32),
                pltpu.SemaphoreType.DMA((steps,)),
                pltpu.SemaphoreType.DMA((2,)),
            ],
        ),
        out_shape=[
            pltpu.VMEM((feat_local, room), BF),
            pltpu.VMEM((STATS, 16, room), BF),
            pltpu.VMEM((WAYS,) + SUMS, F32),
            jax.ShapeDtypeStruct((8,), jnp.int32),
        ],
        compiler_params=pltpu.CompilerParams(vmem_limit_bytes=MOST_VMEM),
        cost_estimate=pl.CostEstimate(flops=4 << 30, bytes_accessed=16 << 20, transcendentals=0),
    )(pos, leaf_of_block, block_rows, codes, gradient.reshape(blocks, BLOCK), hessian.reshape(blocks, BLOCK))


def histogram_kernel(first_rows, info_ref, table_ref, weight_ref, *refs):
    histogram_into(first_rows(info_ref), info_ref, table_ref, weight_ref, refs[:-1], refs[-1])


def histogram_into(starts, info_ref, table_ref, weight_ref, outs, total):
    lane = lax.broadcasted_iota(jnp.int32, (FOLD, WIDTH), 1)
    skew = (lax.broadcasted_iota(jnp.int32, (FOLD, WIDTH), 0) - lane) & (FOLD - 1)

    def product(at, size, fresh):
        half = (lax.broadcasted_iota(jnp.int32, (16, size), 0) >> 3).astype(F32).astype(BF)
        nth = (lax.broadcasted_iota(jnp.int32, (size, 128), 1) >> 3).astype(F32).astype(BF)
        one, zero = jnp.ones((size, 128), BF), jnp.zeros((size, 128), BF)
        none = jnp.zeros((16, size), BF)
        weights = [weight_ref[s, :, pl.ds(at, size)] for s in range(STATS)]
        for way in range(len(starts)):
            both = table_ref[pl.ds(starts[way], PAIR), pl.ds(at, size)].astype(F32)
            for i in range(2):
                code = both[i * FOLD : (i + 1) * FOLD]
                high = jnp.floor(code * (1.0 / LOW))
                low = code - high * LOW
                high = jnp.concatenate([high] * 2, 0).astype(BF) - half
                masks = [high == BF(q) for q in range(0, HIGH, 2)]
                terms = jnp.concatenate([jnp.where(m, w, none) for w in weights for m in masks], 0)
                low = jnp.concatenate([jnp.concatenate([low] * 2, 0).astype(BF)] * 8, 0).T - nth
                picks = jnp.concatenate([jnp.where(low == BF(q), one, zero) for q in (0, 16)], 1)
                sums = lax.dot_general(terms, picks, (((1,), (0,)), ((), ())), preferred_element_type=F32)
                total[2 * way + i] = jnp.where(fresh, 0.0, total[2 * way + i]) + sums

    for leaf in range(LEAVES):
        start = info_ref[2] if leaf else 0
        tiles = info_ref[leaf]
        big = tiles // 4

        @pl.when(tiles == 0)
        def _():
            total[...] = jnp.zeros_like(total)

        @pl.loop(0, big)
        def _(k):
            product(pl.multiple_of(start + k * BIG, BLOCK), BIG, k == 0)

        at = start + big * BIG

        @pl.when((tiles & 2) != 0)
        def _():
            product(pl.multiple_of(at, BLOCK), 2 * TILE, tiles < 4)

        @pl.when((tiles & 1) != 0)
        def _():
            product(pl.multiple_of(at + (tiles & 2) * TILE, BLOCK), TILE, tiles == 1)

        for way in range(len(starts)):
            for i in range(2):
                for s in range(STATS):
                    base = s * ROWS
                    value = total[2 * way + i, base : base + FOLD]
                    for h in range(1, HIGH):
                        piece = total[2 * way + i, base + h * FOLD : base + (h + 1) * FOLD]
                        value = jnp.where(skew == h, pltpu.roll(piece, h, 0), value)
                    outs[way // WAYS][way % WAYS, i, leaf, s] = value


def rows_of(per_owner, jobs):
    def first_rows(info_ref):
        return [
            pl.multiple_of((info_ref[3] ^ way) * per_owner + pair * PAIR, PAIR) for pair, ways in jobs for way in ways
        ]

    return first_rows


def histogram(packed, owners, jobs):
    table, weight, info = packed
    first_rows = rows_of(table.shape[0] // owners, jobs)
    whole = pl.BlockSpec(memory_space=pltpu.VMEM)
    return pl.pallas_call(
        functools.partial(histogram_kernel, first_rows),
        grid_spec=pltpu.PrefetchScalarGridSpec(
            num_scalar_prefetch=1,
            grid=(1,),
            in_specs=[whole, whole],
            out_specs=[whole] * len(jobs),
            scratch_shapes=[pltpu.VMEM((2 * WAYS * len(jobs), DEPTH, WIDTH), F32)],
        ),
        out_shape=[pltpu.VMEM((WAYS,) + SUMS, F32)] * len(jobs),
        compiler_params=pltpu.CompilerParams(vmem_limit_bytes=VMEM_BYTES),
        cost_estimate=pl.CostEstimate(flops=(6 << 30) * len(jobs), bytes_accessed=4 << 20, transcendentals=0),
    )(info, in_vmem(table), in_vmem(weight))


def pick(x, chooser):
    total = 0.0
    for _ in range(3):
        part = x.astype(BF)
        total = total + lax.dot_general(part, chooser, (((1,), (0,)), ((), ())), preferred_element_type=F32)
        x = x - part.astype(F32)
    return total


def gain_kernel(chunks, *refs):
    own, others, gain_ref, top_ref = refs[:chunks], refs[chunks : 2 * chunks], refs[-2], refs[-1]
    before = refs[2 * chunks + 1] if len(refs) > 2 * chunks + 2 else None
    lane = lax.broadcasted_iota(jnp.int32, (FOLD, WIDTH), 1)
    row = lax.broadcasted_iota(jnp.int32, (FOLD, WIDTH), 0)
    rows = lax.broadcasted_iota(jnp.int32, (WIDTH, WIDTH), 0)
    cols = lax.broadcasted_iota(jnp.int32, (WIDTH, WIDTH), 1)

    def chooser(mask):
        return jnp.where(mask, 1.0, 0.0).astype(BF)

    same = (rows & 7) == (cols & 7)
    upto = chooser(same & ((rows >> 3) <= (cols >> 3)))
    same = chooser(same)
    order = chooser(((rows & 7) == (cols >> 5)) & ((rows >> 3) == (cols & 31)))
    apart = (row - (lane >> 5)) & 7
    tops = [jnp.full((FOLD, WIDTH), -jnp.inf, F32)] * LEAVES
    for c in range(chunks):
        pieces = []
        for i in range(2):
            for leaf in range(LEAVES):
                for s in range(STATS):
                    x = own[c][0, i, leaf, s] + others[c][0, i, leaf, s]
                    for bit in (1, 2, 4):
                        x = jnp.where((lane & bit) != 0, pltpu.roll(x, FOLD - bit, 0), x)
                    pieces.append(x)
        stacked = jnp.concatenate(pieces, 0)
        inner = pick(stacked, upto)
        whole = pick(stacked, same)
        gains = []
        for i in range(2):
            for leaf in range(LEAVES):
                left, total = [], []
                for s in range(STATS):
                    at = ((i * LEAVES + leaf) * STATS + s) * FOLD
                    run = whole[at : at + FOLD]
                    for step in (1, 2, 4):
                        run = run + jnp.where(row >= step, pltpu.roll(run, step, 0), 0.0)
                    lower = jnp.where(row >= 1, pltpu.roll(run, 1, 0), 0.0)
                    left.append(inner[at : at + FOLD] + lower)
                    total.append(jnp.broadcast_to(run[FOLD - 1 : FOLD], (FOLD, WIDTH)))
                right = [t - a for t, a in zip(total, left)]
                raw = 0.5 * (
                    left[0] * left[0] / (left[1] + RIDGE)
                    + right[0] * right[0] / (right[1] + RIDGE)
                    - total[0] * total[0] / (total[1] + RIDGE)
                )
                value = jnp.where((left[2] >= MIN_CHILD) & (right[2] >= MIN_CHILD), raw, 0.0)
                gains.append(value)
                tops[leaf] = jnp.maximum(tops[leaf], value)
        z = pick(jnp.concatenate(gains, 0), order)
        for i in range(2):
            for leaf in range(LEAVES):
                at = (i * LEAVES + leaf) * FOLD
                piece = z[at : at + FOLD]
                out = jnp.where(apart == 0, piece, 0.0)
                for d in range(1, FOLD):
                    part = jnp.where(apart == d, piece, 0.0)
                    out = out + pltpu.roll(pltpu.roll(part, FOLD - d, 0), LOW * d, 1)
                gain_ref[leaf, c * PAIR + i * FOLD : c * PAIR + (i + 1) * FOLD, :] = out
    tops = [jnp.max(top, axis=(0, 1), keepdims=True) for top in tops]
    at = lax.broadcasted_iota(jnp.int32, top_ref.shape, 1)
    top = jnp.where(at == 0, tops[0], tops[1])
    top_ref[...] = top if before is None else jnp.maximum(top, before[...])


def gain(own, others, first, features, devices, done):
    count = len(own)
    top = (devices, 128)
    rows = count * PAIR
    return pl.pallas_call(
        functools.partial(gain_kernel, count),
        grid=(1,),
        in_specs=[pl.BlockSpec((1,) + SUMS, lambda i: (0,) * 6)] * (2 * count)
        + ([pl.BlockSpec(memory_space=pl.ANY), pl.BlockSpec(top, lambda i: (0, 0))] if done else []),
        out_specs=[
            pl.BlockSpec((LEAVES, rows, BINS), lambda i: (0, first // count, 0)),
            pl.BlockSpec(top, lambda i: (0, 0)),
        ],
        out_shape=[jax.ShapeDtypeStruct((LEAVES, features, BINS), F32), jax.ShapeDtypeStruct(top, F32)],
        input_output_aliases={2 * count: 0, 2 * count + 1: 1} if done else {},
        compiler_params=pltpu.CompilerParams(vmem_limit_bytes=VMEM_BYTES),
        cost_estimate=pl.CostEstimate(flops=1 << 30, bytes_accessed=1 << 20, transcendentals=0),
    )(*own, *others, *done)


def in_halves(ways, bits):
    if not bits:
        return ways
    return in_halves([w for w in ways if not w & bits[0]], bits[1:]) + in_halves(
        [w for w in ways if w & bits[0]], bits[1:]
    )


def joined(arrays):
    return arrays[0] if len(arrays) == 1 else jnp.concatenate(arrays, 0)


def in_turn(packed, done):
    return (*packed[:2], lax.optimization_barrier((packed[2], *done))[0])


def local(owners, devices, bin_codes, gradient, hessian, leaf_of_block, block_rows):
    row_total, feat_local = bin_codes.shape
    pos = lax.axis_index("rows").astype(jnp.int32)[None]
    room = -(-(row_total + 2 * TILE + BLOCK) // SPAN) * SPAN
    pairs = feat_local // owners // PAIR
    bits = [1 << b for b in range(1, owners.bit_length() - 1)]
    kept = in_halves([w for w in range(owners) if not w & 1], bits)
    parts = [kept[i : i + WAYS] for i in range(0, len(kept), WAYS)]

    def swap(x, bit):
        return lax.ppermute(x, "rows", [(i, i ^ bit) for i in range(owners)])

    def ways_of(side, part):
        return [w ^ side for w in part]

    first_rows = rows_of(feat_local // owners, [(0, ways_of(1, parts[0]))])
    *packed, first, info = pack(
        pos, leaf_of_block, block_rows, bin_codes, gradient, hessian, room, first_rows
    )
    packed = (*packed, info)
    keep, other, left = {}, {0: [swap(first, 1)]}, {pair: bits for pair in range(pairs)}
    plan = PLAN
    if pairs != 4:
        plan = [([(pair, side)], []) for pair in range(pairs) for side in (1, 0)]
        plan += [([], [pair for pair in range(pairs) for _ in bits])]
    for jobs, exchanges in plan:
        for n, part in enumerate(parts):
            todo = [job for job in jobs if n or job != (0, 1)]
            if not todo:
                continue
            sums = histogram(packed, owners, [(pair, ways_of(side, part)) for pair, side in todo])
            for (pair, side), x in zip(todo, sums):
                (other if side else keep).setdefault(pair, []).append(swap(x, 1) if side else x)
            packed = in_turn(packed, sums)
        moved = []
        for pair in exchanges:
            if isinstance(keep[pair], list):
                keep[pair], other[pair] = joined(keep[pair]), joined(other[pair])
            mine, theirs, (bit, *left[pair]) = keep[pair], other[pair], left[pair]
            half = mine.shape[0] // 2
            on = mine[half:] + theirs[half:]
            moved.append(on)
            keep[pair], other[pair] = mine[:half] + theirs[:half], swap(on, bit)
        packed = in_turn(packed, moved)
    done = ()
    for group in (range(pairs - 1), range(pairs - 1, pairs)):
        if group:
            done = gain(
                [keep[p] for p in group], [other[p] for p in group], group[0], feat_local // owners, devices, done
            )
    split_gain, best = done
    best = lax.all_to_all(best, ("rows", "feat"), 0, 0, tiled=True)
    return split_gain, jnp.max(best, axis=0)[:LEAVES]


def solution(mesh):
    return jax.shard_map(
        functools.partial(local, mesh.shape["rows"], mesh.size),
        mesh=mesh,
        in_specs=(P("rows", "feat"), P("rows"), P("rows"), P("rows"), P("rows")),
        out_specs=(P(None, ("feat", "rows"), None), P()),
        check_vma=False,
    )
```

```python
import functools

import jax
import jax.numpy as jnp
from jax import lax
from jax.experimental import pallas as pl
from jax.experimental.pallas import tpu as pltpu
from jax.sharding import PartitionSpec as P

BINS = 256
LEAVES = 2
BLOCK = 128
MIN_CHILD = 20
RIDGE = 1.0

STATS = 3
HIGH = 8
LOW = 32
FOLD = 8
PAIR = 2 * FOLD
WIDTH = LOW * FOLD
ROWS = HIGH * FOLD
DEPTH = STATS * ROWS
TILE = 256
BIG = 3 * TILE
SPAN = 512
WAYS = 4
PLAN = (([(1,1),(2,1)], []), ([(3,1),(0,0)], [0]), ([(2,0),(1,0)], [2,0]), ([(3,0)], [1,2]), ([], [3,1,3]))
SUMS = (2, LEAVES, STATS, FOLD, WIDTH)

BF = jnp.bfloat16
F32 = jnp.float32
VMEM_BYTES = 24 << 20
MOST_VMEM = 54 << 20


def nt(a, b):
    return lax.dot_general(a, b, (((1,), (1,)), ((), ())), preferred_element_type=F32)


def in_vmem(x):
    return pltpu.with_memory_space_constraint(x, pltpu.VMEM)


def live_up(count):
    return (count + 15) // 16 * 16


def tiles_of(total):
    return (total + TILE - 1) // TILE


def pack_kernel(
    blocks, first_rows,
    pos_ref, leaf_ref, rows_ref, codes_ref, grad_ref, hess_ref,
    table_ref, weight_ref, sums_ref, info_ref,
    arrived, held, rows_held, pair_held, total, offset, ends, in_sem, pair_sem,
):
    steps = blocks * BLOCK // SPAN
    per_step = SPAN // BLOCK
    feats = held.shape[1]

    def fetch(i):
        return pltpu.make_async_copy(
            codes_ref.at[pl.ds(pl.multiple_of(i * SPAN, SPAN), SPAN), :], arrived.at[i], in_sem.at[i]
        )

    pairs = [
        pltpu.make_async_copy(ref, pair_held.at[i], pair_sem.at[i]) for i, ref in enumerate((grad_ref, hess_ref))
    ]
    for copy in pairs:
        copy.start()
    for i in range(steps):
        fetch(i).start()

    def count(k, room):
        size, leaf = live_up(rows_ref[k]), leaf_ref[k]
        return room[0] + size * (1 - leaf), room[1] + size * leaf

    first, second = lax.fori_loop(0, blocks, count, (0, 0), unroll=4)
    start = tiles_of(first) * TILE + BLOCK

    def place(k, room):
        offset[k] = jnp.where(leaf_ref[k] == 0, room[0], room[1])
        room = count(k, room)
        ends[0, k], ends[1, k] = room
        return room

    lax.fori_loop(0, blocks, place, (0, start), unroll=4)
    info_ref[0] = tiles_of(first)
    info_ref[1] = tiles_of(second)
    info_ref[2] = start
    info_ref[3] = pos_ref[0]

    rows_held[...] = jnp.zeros_like(rows_held)
    for copy in pairs:
        copy.wait()
    grads, hessians = pair_held[0].astype(F32), pair_held[1].astype(F32)
    lane = lax.broadcasted_iota(jnp.int32, (8, BLOCK), 1)
    row = lax.broadcasted_iota(jnp.int32, (8, BLOCK), 0)
    rolled = []
    for k in range(blocks):
        grad = jnp.broadcast_to(grads[k : k + 1], (8, BLOCK))
        hess = jnp.broadcast_to(hessians[k : k + 1], (8, BLOCK))
        value = jnp.where(row == 0, grad, jnp.where(row == 1, hess, jnp.where(row == 2, 1.0, 0.0)))
        value = jnp.where(lane < rows_ref[k], value, 0.0)
        rolled.append(pltpu.roll(value, lax.rem(offset[k], BLOCK), 1))
    for k in range(blocks):
        at = offset[k]
        shift = lax.rem(at, BLOCK)
        tile = pl.multiple_of(at - shift, BLOCK)
        here = rows_held[:, pl.ds(tile, BLOCK)]
        rows_held[:, pl.ds(tile, BLOCK)] = jnp.where(lane < shift, here, rolled[k])
        after = pl.ds(pl.multiple_of(tile + BLOCK, BLOCK), BLOCK)
        rows_held[:, after] = jnp.where(lane < shift, rolled[k], 0.0)

    size = 256
    eye = (
        lax.broadcasted_iota(jnp.int32, (size, size), 0) == lax.broadcasted_iota(jnp.int32, (size, size), 1)
    ).astype(F32).astype(BF)

    def turn(base, tiles, done):
        @pl.loop(done, tiles)
        def _(j):
            at = pl.multiple_of(base + j * TILE, BLOCK)
            for f in range(0, feats, size):
                table_ref[f : f + size, pl.ds(at, TILE)] = nt(eye, held[pl.ds(at, TILE), f : f + size]).astype(BF)
            for s in range(STATS):
                weight_ref[s, :, pl.ds(at, TILE)] = jnp.broadcast_to(
                    rows_held[s : s + 1, pl.ds(at, TILE)], (16, TILE)
                ).astype(BF)

        return jnp.maximum(done, tiles)

    def step(i, done):
        fetch(i).wait()
        for j in range(per_step):
            at = pl.multiple_of(offset[i * per_step + j], 16)
            held[pl.ds(at, BLOCK), :] = arrived[i, j * BLOCK : (j + 1) * BLOCK, :].astype(F32).astype(BF)
        last = (i + 1) * per_step - 1
        return (
            turn(0, ends[0, last] // TILE, done[0]),
            turn(start, (ends[1, last] - start) // TILE, done[1]),
        )

    done = lax.fori_loop(0, steps, step, (0, 0))
    turn(0, tiles_of(first), done[0])
    turn(start, tiles_of(second), done[1])
    histogram_into(first_rows(info_ref), info_ref, table_ref, weight_ref, [sums_ref], total)


def pack(pos, leaf_of_block, block_rows, codes, gradient, hessian, room, first_rows):
    row_total, feat_local = codes.shape
    blocks = row_total // BLOCK
    steps = row_total // SPAN
    whole, anywhere = pl.BlockSpec(memory_space=pltpu.VMEM), pl.BlockSpec(memory_space=pl.ANY)
    return pl.pallas_call(
        functools.partial(pack_kernel, blocks, first_rows),
        grid_spec=pltpu.PrefetchScalarGridSpec(
            num_scalar_prefetch=3,
            grid=(1,),
            in_specs=[anywhere] * 3,
            out_specs=[whole, whole, whole, pl.BlockSpec(memory_space=pltpu.SMEM)],
            scratch_shapes=[
                pltpu.VMEM((steps, SPAN, feat_local), jnp.int32),
                pltpu.VMEM((room, feat_local), BF),
                pltpu.VMEM((8, room), F32),
                pltpu.VMEM((2, blocks, BLOCK), BF),
                pltpu.VMEM((2 * WAYS, DEPTH, WIDTH), F32),
                pltpu.SMEM((blocks,), jnp.int32),
                pltpu.SMEM((2, blocks), jnp.int32),
                pltpu.SemaphoreType.DMA((steps,)),
                pltpu.SemaphoreType.DMA((2,)),
            ],
        ),
        out_shape=[
            pltpu.VMEM((feat_local, room), BF),
            pltpu.VMEM((STATS, 16, room), BF),
            pltpu.VMEM((WAYS,) + SUMS, F32),
            jax.ShapeDtypeStruct((8,), jnp.int32),
        ],
        compiler_params=pltpu.CompilerParams(vmem_limit_bytes=MOST_VMEM),
        cost_estimate=pl.CostEstimate(flops=4 << 30, bytes_accessed=16 << 20, transcendentals=0),
    )(pos, leaf_of_block, block_rows, codes, gradient.reshape(blocks, BLOCK), hessian.reshape(blocks, BLOCK))


def histogram_kernel(first_rows, info_ref, table_ref, weight_ref, *refs):
    histogram_into(first_rows(info_ref), info_ref, table_ref, weight_ref, refs[:-1], refs[-1])


def histogram_into(starts, info_ref, table_ref, weight_ref, outs, total):
    lane = lax.broadcasted_iota(jnp.int32, (FOLD, WIDTH), 1)
    skew = (lax.broadcasted_iota(jnp.int32, (FOLD, WIDTH), 0) - lane) & (FOLD - 1)

    def product(at, size, fresh):
        half = (lax.broadcasted_iota(jnp.int32, (16, size), 0) >> 3).astype(F32).astype(BF)
        nth = (lax.broadcasted_iota(jnp.int32, (size, 128), 1) >> 3).astype(F32).astype(BF)
        one, zero = jnp.ones((size, 128), BF), jnp.zeros((size, 128), BF)
        none = jnp.zeros((16, size), BF)
        weights = [weight_ref[s, :, pl.ds(at, size)] for s in range(STATS)]
        for way in range(len(starts)):
            both = table_ref[pl.ds(starts[way], PAIR), pl.ds(at, size)].astype(F32)
            for i in range(2):
                code = both[i * FOLD : (i + 1) * FOLD]
                high = jnp.floor(code * (1.0 / LOW))
                low = code - high * LOW
                high = jnp.concatenate([high] * 2, 0).astype(BF) - half
                masks = [high == BF(q) for q in range(0, HIGH, 2)]
                terms = jnp.concatenate([jnp.where(m, w, none) for w in weights for m in masks], 0)
                low = jnp.concatenate([jnp.concatenate([low] * 2, 0).astype(BF)] * 8, 0).T - nth
                picks = jnp.concatenate([jnp.where(low == BF(q), one, zero) for q in (0, 16)], 1)
                sums = lax.dot_general(terms, picks, (((1,), (0,)), ((), ())), preferred_element_type=F32)
                total[2 * way + i] = jnp.where(fresh, 0.0, total[2 * way + i]) + sums

    for leaf in range(LEAVES):
        start = info_ref[2] if leaf else 0
        tiles = info_ref[leaf]
        big = tiles // 3
        rest = tiles - 3 * big

        @pl.when(tiles == 0)
        def _():
            total[...] = jnp.zeros_like(total)

        @pl.loop(0, big)
        def _(k):
            product(pl.multiple_of(start + k * BIG, BLOCK), BIG, k == 0)

        at = start + big * BIG

        @pl.when(rest == 2)
        def _():
            product(pl.multiple_of(at, BLOCK), 2 * TILE, tiles == 2)

        @pl.when(rest == 1)
        def _():
            product(pl.multiple_of(at, BLOCK), TILE, tiles == 1)

        for way in range(len(starts)):
            for i in range(2):
                for s in range(STATS):
                    base = s * ROWS
                    value = total[2 * way + i, base : base + FOLD]
                    for h in range(1, HIGH):
                        piece = total[2 * way + i, base + h * FOLD : base + (h + 1) * FOLD]
                        value = jnp.where(skew == h, pltpu.roll(piece, h, 0), value)
                    outs[way // WAYS][way % WAYS, i, leaf, s] = value


def rows_of(per_owner, jobs):
    def first_rows(info_ref):
        return [
            pl.multiple_of((info_ref[3] ^ way) * per_owner + pair * PAIR, PAIR) for pair, ways in jobs for way in ways
        ]

    return first_rows


def histogram(packed, owners, jobs):
    table, weight, info = packed
    first_rows = rows_of(table.shape[0] // owners, jobs)
    whole = pl.BlockSpec(memory_space=pltpu.VMEM)
    return pl.pallas_call(
        functools.partial(histogram_kernel, first_rows),
        grid_spec=pltpu.PrefetchScalarGridSpec(
            num_scalar_prefetch=1,
            grid=(1,),
            in_specs=[whole, whole],
            out_specs=[whole] * len(jobs),
            scratch_shapes=[pltpu.VMEM((2 * WAYS * len(jobs), DEPTH, WIDTH), F32)],
        ),
        out_shape=[pltpu.VMEM((WAYS,) + SUMS, F32)] * len(jobs),
        compiler_params=pltpu.CompilerParams(vmem_limit_bytes=VMEM_BYTES),
        cost_estimate=pl.CostEstimate(flops=(6 << 30) * len(jobs), bytes_accessed=4 << 20, transcendentals=0),
    )(info, in_vmem(table), in_vmem(weight))


def pick(x, chooser):
    total = 0.0
    for _ in range(3):
        part = x.astype(BF)
        total = total + lax.dot_general(part, chooser, (((1,), (0,)), ((), ())), preferred_element_type=F32)
        x = x - part.astype(F32)
    return total


def gain_kernel(chunks, *refs):
    own, others, gain_ref, top_ref = refs[:chunks], refs[chunks : 2 * chunks], refs[-2], refs[-1]
    before = refs[2 * chunks + 1] if len(refs) > 2 * chunks + 2 else None
    lane = lax.broadcasted_iota(jnp.int32, (FOLD, WIDTH), 1)
    row = lax.broadcasted_iota(jnp.int32, (FOLD, WIDTH), 0)
    rows = lax.broadcasted_iota(jnp.int32, (WIDTH, WIDTH), 0)
    cols = lax.broadcasted_iota(jnp.int32, (WIDTH, WIDTH), 1)

    def chooser(mask):
        return jnp.where(mask, 1.0, 0.0).astype(BF)

    same = (rows & 7) == (cols & 7)
    upto = chooser(same & ((rows >> 3) <= (cols >> 3)))
    same = chooser(same)
    order = chooser(((rows & 7) == (cols >> 5)) & ((rows >> 3) == (cols & 31)))
    apart = (row - (lane >> 5)) & 7
    tops = [jnp.full((FOLD, WIDTH), -jnp.inf, F32)] * LEAVES
    for c in range(chunks):
        pieces = []
        for i in range(2):
            for leaf in range(LEAVES):
                for s in range(STATS):
                    x = own[c][0, i, leaf, s] + others[c][0, i, leaf, s]
                    for bit in (1, 2, 4):
                        x = jnp.where((lane & bit) != 0, pltpu.roll(x, FOLD - bit, 0), x)
                    pieces.append(x)
        stacked = jnp.concatenate(pieces, 0)
        inner = pick(stacked, upto)
        whole = pick(stacked, same)
        gains = []
        for i in range(2):
            for leaf in range(LEAVES):
                left, total = [], []
                for s in range(STATS):
                    at = ((i * LEAVES + leaf) * STATS + s) * FOLD
                    run = whole[at : at + FOLD]
                    for step in (1, 2, 4):
                        run = run + jnp.where(row >= step, pltpu.roll(run, step, 0), 0.0)
                    lower = jnp.where(row >= 1, pltpu.roll(run, 1, 0), 0.0)
                    left.append(inner[at : at + FOLD] + lower)
                    total.append(jnp.broadcast_to(run[FOLD - 1 : FOLD], (FOLD, WIDTH)))
                right = [t - a for t, a in zip(total, left)]
                raw = 0.5 * (
                    left[0] * left[0] / (left[1] + RIDGE)
                    + right[0] * right[0] / (right[1] + RIDGE)
                    - total[0] * total[0] / (total[1] + RIDGE)
                )
                value = jnp.where((left[2] >= MIN_CHILD) & (right[2] >= MIN_CHILD), raw, 0.0)
                gains.append(value)
                tops[leaf] = jnp.maximum(tops[leaf], value)
        z = pick(jnp.concatenate(gains, 0), order)
        for i in range(2):
            for leaf in range(LEAVES):
                at = (i * LEAVES + leaf) * FOLD
                piece = z[at : at + FOLD]
                out = jnp.where(apart == 0, piece, 0.0)
                for d in range(1, FOLD):
                    part = jnp.where(apart == d, piece, 0.0)
                    out = out + pltpu.roll(pltpu.roll(part, FOLD - d, 0), LOW * d, 1)
                gain_ref[leaf, c * PAIR + i * FOLD : c * PAIR + (i + 1) * FOLD, :] = out
    tops = [jnp.max(top, axis=(0, 1), keepdims=True) for top in tops]
    at = lax.broadcasted_iota(jnp.int32, top_ref.shape, 1)
    top = jnp.where(at == 0, tops[0], tops[1])
    top_ref[...] = top if before is None else jnp.maximum(top, before[...])


def gain(own, others, first, features, devices, done):
    count = len(own)
    top = (devices, 128)
    rows = count * PAIR
    return pl.pallas_call(
        functools.partial(gain_kernel, count),
        grid=(1,),
        in_specs=[pl.BlockSpec((1,) + SUMS, lambda i: (0,) * 6)] * (2 * count)
        + ([pl.BlockSpec(memory_space=pl.ANY), pl.BlockSpec(top, lambda i: (0, 0))] if done else []),
        out_specs=[
            pl.BlockSpec((LEAVES, rows, BINS), lambda i: (0, first // count, 0)),
            pl.BlockSpec(top, lambda i: (0, 0)),
        ],
        out_shape=[jax.ShapeDtypeStruct((LEAVES, features, BINS), F32), jax.ShapeDtypeStruct(top, F32)],
        input_output_aliases={2 * count: 0, 2 * count + 1: 1} if done else {},
        compiler_params=pltpu.CompilerParams(vmem_limit_bytes=VMEM_BYTES),
        cost_estimate=pl.CostEstimate(flops=1 << 30, bytes_accessed=1 << 20, transcendentals=0),
    )(*own, *others, *done)


def in_halves(ways, bits):
    if not bits:
        return ways
    return in_halves([w for w in ways if not w & bits[0]], bits[1:]) + in_halves(
        [w for w in ways if w & bits[0]], bits[1:]
    )


def joined(arrays):
    return arrays[0] if len(arrays) == 1 else jnp.concatenate(arrays, 0)


def in_turn(packed, done):
    return (*packed[:2], lax.optimization_barrier((packed[2], *done))[0])


def local(owners, devices, bin_codes, gradient, hessian, leaf_of_block, block_rows):
    row_total, feat_local = bin_codes.shape
    pos = lax.axis_index("rows").astype(jnp.int32)[None]
    room = -(-(row_total + 2 * TILE + BLOCK) // SPAN) * SPAN
    pairs = feat_local // owners // PAIR
    bits = [1 << b for b in range(1, owners.bit_length() - 1)]
    kept = in_halves([w for w in range(owners) if not w & 1], bits)
    parts = [kept[i : i + WAYS] for i in range(0, len(kept), WAYS)]

    def swap(x, bit):
        return lax.ppermute(x, "rows", [(i, i ^ bit) for i in range(owners)])

    def ways_of(side, part):
        return [w ^ side for w in part]

    first_rows = rows_of(feat_local // owners, [(0, ways_of(1, parts[0]))])
    *packed, first, info = pack(
        pos, leaf_of_block, block_rows, bin_codes, gradient, hessian, room, first_rows
    )
    packed = (*packed, info)
    keep, other, left = {}, {0: [swap(first, 1)]}, {pair: bits for pair in range(pairs)}
    plan = PLAN
    if pairs != 4:
        plan = [([(pair, side)], []) for pair in range(pairs) for side in (1, 0)]
        plan += [([], [pair for pair in range(pairs) for _ in bits])]
    for jobs, exchanges in plan:
        for n, part in enumerate(parts):
            todo = [job for job in jobs if n or job != (0, 1)]
            if not todo:
                continue
            sums = histogram(packed, owners, [(pair, ways_of(side, part)) for pair, side in todo])
            for (pair, side), x in zip(todo, sums):
                (other if side else keep).setdefault(pair, []).append(swap(x, 1) if side else x)
            packed = in_turn(packed, sums)
        moved = []
        for pair in exchanges:
            if isinstance(keep[pair], list):
                keep[pair], other[pair] = joined(keep[pair]), joined(other[pair])
            mine, theirs, (bit, *left[pair]) = keep[pair], other[pair], left[pair]
            half = mine.shape[0] // 2
            on = mine[half:] + theirs[half:]
            moved.append(on)
            keep[pair], other[pair] = mine[:half] + theirs[:half], swap(on, bit)
        packed = in_turn(packed, moved)
    done = ()
    for group in (range(pairs - 1), range(pairs - 1, pairs)):
        if group:
            done = gain(
                [keep[p] for p in group], [other[p] for p in group], group[0], feat_local // owners, devices, done
            )
    split_gain, best = done
    best = lax.all_to_all(best, ("rows", "feat"), 0, 0, tiled=True)
    return split_gain, jnp.max(best, axis=0)[:LEAVES]


def solution(mesh):
    return jax.shard_map(
        functools.partial(local, mesh.shape["rows"], mesh.size),
        mesh=mesh,
        in_specs=(P("rows", "feat"), P("rows"), P("rows"), P("rows"), P("rows")),
        out_specs=(P(None, ("feat", "rows"), None), P()),
        check_vma=False,
    )
```

```python
import functools

import jax
import jax.numpy as jnp
from jax import lax
from jax.experimental import pallas as pl
from jax.experimental.pallas import tpu as pltpu
from jax.sharding import PartitionSpec as P

BINS = 256
LEAVES = 2
BLOCK = 128
MIN_CHILD = 20
RIDGE = 1.0

STATS = 3
HIGH = 8
LOW = 32
FOLD = 8
PAIR = 2 * FOLD
WIDTH = LOW * FOLD
ROWS = HIGH * FOLD
DEPTH = STATS * ROWS
TILE = 256
BIG = 3 * TILE
SPAN = 512
WAYS = 4
ORDERS = ((2, 4, 1), (1, 2, 4), (1, 2, 4), (1, 2, 4))
PLAN = (
    ([(1, 1), (2, 1)], []),
    ([(0, 0), (1, 0)], [0, 1]),
    ([(3, 1), (2, 0)], [1, 2, 0]),
    ([(3, 0)], [2, 3]),
    ([], [3]),
)
SUMS = (2, LEAVES, STATS, FOLD, WIDTH)

BF = jnp.bfloat16
F32 = jnp.float32
VMEM_BYTES = 24 << 20
MOST_VMEM = 54 << 20


def nt(a, b):
    return lax.dot_general(a, b, (((1,), (1,)), ((), ())), preferred_element_type=F32)


def in_vmem(x):
    return pltpu.with_memory_space_constraint(x, pltpu.VMEM)


def live_up(count):
    return (count + 15) // 16 * 16


def tiles_of(total):
    return (total + TILE - 1) // TILE


def pack_kernel(
    blocks, first_rows,
    pos_ref, leaf_ref, rows_ref, codes_ref, grad_ref, hess_ref,
    table_ref, weight_ref, sums_ref, info_ref,
    arrived, held, rows_held, pair_held, total, offset, ends, in_sem, pair_sem,
):
    steps = blocks * BLOCK // SPAN
    per_step = SPAN // BLOCK
    feats = held.shape[1]

    def fetch(i):
        return pltpu.make_async_copy(
            codes_ref.at[pl.ds(pl.multiple_of(i * SPAN, SPAN), SPAN), :], arrived.at[i], in_sem.at[i]
        )

    pairs = [
        pltpu.make_async_copy(ref, pair_held.at[i], pair_sem.at[i]) for i, ref in enumerate((grad_ref, hess_ref))
    ]
    for copy in pairs:
        copy.start()
    for i in range(steps):
        fetch(i).start()

    def count(k, room):
        size, leaf = live_up(rows_ref[k]), leaf_ref[k]
        return room[0] + size * (1 - leaf), room[1] + size * leaf

    first, second = lax.fori_loop(0, blocks, count, (0, 0), unroll=4)
    start = tiles_of(first) * TILE + BLOCK

    def place(k, room):
        offset[k] = jnp.where(leaf_ref[k] == 0, room[0], room[1])
        room = count(k, room)
        ends[0, k], ends[1, k] = room
        return room

    lax.fori_loop(0, blocks, place, (0, start), unroll=4)
    info_ref[0] = tiles_of(first)
    info_ref[1] = tiles_of(second)
    info_ref[2] = start
    info_ref[3] = pos_ref[0]

    rows_held[...] = jnp.zeros_like(rows_held)
    for copy in pairs:
        copy.wait()
    grads, hessians = pair_held[0].astype(F32), pair_held[1].astype(F32)
    lane = lax.broadcasted_iota(jnp.int32, (8, BLOCK), 1)
    row = lax.broadcasted_iota(jnp.int32, (8, BLOCK), 0)
    rolled = []
    for k in range(blocks):
        grad = jnp.broadcast_to(grads[k : k + 1], (8, BLOCK))
        hess = jnp.broadcast_to(hessians[k : k + 1], (8, BLOCK))
        value = jnp.where(row == 0, grad, jnp.where(row == 1, hess, jnp.where(row == 2, 1.0, 0.0)))
        value = jnp.where(lane < rows_ref[k], value, 0.0)
        rolled.append(pltpu.roll(value, lax.rem(offset[k], BLOCK), 1))
    for k in range(blocks):
        at = offset[k]
        shift = lax.rem(at, BLOCK)
        tile = pl.multiple_of(at - shift, BLOCK)
        here = rows_held[:, pl.ds(tile, BLOCK)]
        rows_held[:, pl.ds(tile, BLOCK)] = jnp.where(lane < shift, here, rolled[k])
        after = pl.ds(pl.multiple_of(tile + BLOCK, BLOCK), BLOCK)
        rows_held[:, after] = jnp.where(lane < shift, rolled[k], 0.0)

    size = 256
    eye = (
        lax.broadcasted_iota(jnp.int32, (size, size), 0) == lax.broadcasted_iota(jnp.int32, (size, size), 1)
    ).astype(F32).astype(BF)

    def turn(base, tiles, done):
        @pl.loop(done, tiles)
        def _(j):
            at = pl.multiple_of(base + j * TILE, BLOCK)
            for f in range(0, feats, size):
                table_ref[f : f + size, pl.ds(at, TILE)] = nt(eye, held[pl.ds(at, TILE), f : f + size]).astype(BF)
            for s in range(STATS):
                weight_ref[s, :, pl.ds(at, TILE)] = jnp.broadcast_to(
                    rows_held[s : s + 1, pl.ds(at, TILE)], (16, TILE)
                ).astype(BF)

        return jnp.maximum(done, tiles)

    def step(i, done):
        fetch(i).wait()
        for j in range(per_step):
            at = pl.multiple_of(offset[i * per_step + j], 16)
            held[pl.ds(at, BLOCK), :] = arrived[i, j * BLOCK : (j + 1) * BLOCK, :].astype(F32).astype(BF)
        last = (i + 1) * per_step - 1
        return (
            turn(0, ends[0, last] // TILE, done[0]),
            turn(start, (ends[1, last] - start) // TILE, done[1]),
        )

    done = lax.fori_loop(0, steps, step, (0, 0))
    turn(0, tiles_of(first), done[0])
    turn(start, tiles_of(second), done[1])
    histogram_into(first_rows(info_ref), info_ref, table_ref, weight_ref, [sums_ref], total)


def pack(pos, leaf_of_block, block_rows, codes, gradient, hessian, room, first_rows):
    row_total, feat_local = codes.shape
    blocks = row_total // BLOCK
    steps = row_total // SPAN
    whole, anywhere = pl.BlockSpec(memory_space=pltpu.VMEM), pl.BlockSpec(memory_space=pl.ANY)
    return pl.pallas_call(
        functools.partial(pack_kernel, blocks, first_rows),
        grid_spec=pltpu.PrefetchScalarGridSpec(
            num_scalar_prefetch=3,
            grid=(1,),
            in_specs=[anywhere] * 3,
            out_specs=[whole, whole, whole, pl.BlockSpec(memory_space=pltpu.SMEM)],
            scratch_shapes=[
                pltpu.VMEM((steps, SPAN, feat_local), jnp.int32),
                pltpu.VMEM((room, feat_local), BF),
                pltpu.VMEM((8, room), F32),
                pltpu.VMEM((2, blocks, BLOCK), BF),
                pltpu.VMEM((2 * WAYS, DEPTH, WIDTH), F32),
                pltpu.SMEM((blocks,), jnp.int32),
                pltpu.SMEM((2, blocks), jnp.int32),
                pltpu.SemaphoreType.DMA((steps,)),
                pltpu.SemaphoreType.DMA((2,)),
            ],
        ),
        out_shape=[
            pltpu.VMEM((feat_local, room), BF),
            pltpu.VMEM((STATS, 16, room), BF),
            pltpu.VMEM((WAYS,) + SUMS, F32),
            pltpu.SMEM((8,), jnp.int32),
        ],
        compiler_params=pltpu.CompilerParams(vmem_limit_bytes=MOST_VMEM),
        cost_estimate=pl.CostEstimate(flops=4 << 30, bytes_accessed=16 << 20, transcendentals=0),
    )(pos, leaf_of_block, block_rows, codes, gradient.reshape(blocks, BLOCK), hessian.reshape(blocks, BLOCK))


def histogram_kernel(first_rows, info_ref, table_ref, weight_ref, *refs):
    histogram_into(first_rows(info_ref), info_ref, table_ref, weight_ref, refs[:-1], refs[-1])


def histogram_into(starts, info_ref, table_ref, weight_ref, outs, total):
    lane = lax.broadcasted_iota(jnp.int32, (FOLD, WIDTH), 1)
    skew = (lax.broadcasted_iota(jnp.int32, (FOLD, WIDTH), 0) - lane) & (FOLD - 1)

    def product(at, size, fresh):
        half = (lax.broadcasted_iota(jnp.int32, (16, size), 0) >> 3).astype(F32).astype(BF)
        nth = (lax.broadcasted_iota(jnp.int32, (size, 128), 1) >> 3).astype(F32).astype(BF)
        one, zero = jnp.ones((size, 128), BF), jnp.zeros((size, 128), BF)
        none = jnp.zeros((16, size), BF)
        weights = [weight_ref[s, :, pl.ds(at, size)] for s in range(STATS)]
        for way in range(len(starts)):
            both = table_ref[pl.ds(starts[way], PAIR), pl.ds(at, size)].astype(F32)
            for i in range(2):
                code = both[i * FOLD : (i + 1) * FOLD]
                high = jnp.floor(code * (1.0 / LOW))
                low = code - high * LOW
                high = jnp.concatenate([high] * 2, 0).astype(BF) - half
                masks = [high == BF(q) for q in range(0, HIGH, 2)]
                terms = jnp.concatenate([jnp.where(m, w, none) for w in weights for m in masks], 0)
                low = jnp.concatenate([jnp.concatenate([low] * 2, 0).astype(BF)] * 8, 0).T - nth
                picks = jnp.concatenate([jnp.where(low == BF(q), one, zero) for q in (0, 16)], 1)
                sums = lax.dot_general(terms, picks, (((1,), (0,)), ((), ())), preferred_element_type=F32)
                total[2 * way + i] = jnp.where(fresh, 0.0, total[2 * way + i]) + sums

    for leaf in range(LEAVES):
        start = info_ref[2] if leaf else 0
        tiles = info_ref[leaf]
        big = tiles // 3
        rest = tiles - 3 * big

        @pl.when(tiles == 0)
        def _():
            total[...] = jnp.zeros_like(total)

        @pl.loop(0, big)
        def _(k):
            product(pl.multiple_of(start + k * BIG, BLOCK), BIG, k == 0)

        at = start + big * BIG

        @pl.when(rest == 2)
        def _():
            product(pl.multiple_of(at, BLOCK), 2 * TILE, tiles == 2)

        @pl.when(rest == 1)
        def _():
            product(pl.multiple_of(at, BLOCK), TILE, tiles == 1)

        for way in range(len(starts)):
            for i in range(2):
                for s in range(STATS):
                    base = s * ROWS
                    value = total[2 * way + i, base : base + FOLD]
                    for h in range(1, HIGH):
                        piece = total[2 * way + i, base + h * FOLD : base + (h + 1) * FOLD]
                        value = jnp.where(skew == h, pltpu.roll(piece, h, 0), value)
                    outs[way // WAYS][way % WAYS, i, leaf, s] = value


def rows_of(per_owner, jobs):
    def first_rows(info_ref):
        return [
            pl.multiple_of((info_ref[3] ^ way) * per_owner + pair * PAIR, PAIR) for pair, ways in jobs for way in ways
        ]

    return first_rows


def histogram(packed, owners, jobs):
    table, weight, info = packed
    first_rows = rows_of(table.shape[0] // owners, jobs)
    whole = pl.BlockSpec(memory_space=pltpu.VMEM)
    return pl.pallas_call(
        functools.partial(histogram_kernel, first_rows),
        grid_spec=pltpu.PrefetchScalarGridSpec(
            num_scalar_prefetch=1,
            grid=(1,),
            in_specs=[whole, whole],
            out_specs=[whole] * len(jobs),
            scratch_shapes=[pltpu.VMEM((2 * WAYS * len(jobs), DEPTH, WIDTH), F32)],
        ),
        out_shape=[pltpu.VMEM((WAYS,) + SUMS, F32)] * len(jobs),
        compiler_params=pltpu.CompilerParams(vmem_limit_bytes=VMEM_BYTES),
        cost_estimate=pl.CostEstimate(flops=(6 << 30) * len(jobs), bytes_accessed=4 << 20, transcendentals=0),
    )(pltpu.with_memory_space_constraint(info, pltpu.SMEM), in_vmem(table), in_vmem(weight))


def pick(x, chooser):
    total = 0.0
    for _ in range(3):
        part = x.astype(BF)
        total = total + lax.dot_general(part, chooser, (((1,), (0,)), ((), ())), preferred_element_type=F32)
        x = x - part.astype(F32)
    return total


def gain_kernel(chunks, *refs):
    own, others, gain_ref, top_ref = refs[:chunks], refs[chunks : 2 * chunks], refs[-2], refs[-1]
    before = refs[2 * chunks + 1] if len(refs) > 2 * chunks + 2 else None
    lane = lax.broadcasted_iota(jnp.int32, (FOLD, WIDTH), 1)
    row = lax.broadcasted_iota(jnp.int32, (FOLD, WIDTH), 0)
    rows = lax.broadcasted_iota(jnp.int32, (WIDTH, WIDTH), 0)
    cols = lax.broadcasted_iota(jnp.int32, (WIDTH, WIDTH), 1)

    def chooser(mask):
        return jnp.where(mask, 1.0, 0.0).astype(BF)

    same = (rows & 7) == (cols & 7)
    upto = chooser(same & ((rows >> 3) <= (cols >> 3)))
    same = chooser(same)
    order = chooser(((rows & 7) == (cols >> 5)) & ((rows >> 3) == (cols & 31)))
    apart = (row - (lane >> 5)) & 7
    tops = [jnp.full((FOLD, WIDTH), -jnp.inf, F32)] * LEAVES
    for c in range(chunks):
        pieces = []
        for i in range(2):
            for leaf in range(LEAVES):
                for s in range(STATS):
                    x = own[c][0, i, leaf, s] + others[c][0, i, leaf, s]
                    for bit in (1, 2, 4):
                        x = jnp.where((lane & bit) != 0, pltpu.roll(x, FOLD - bit, 0), x)
                    pieces.append(x)
        stacked = jnp.concatenate(pieces, 0)
        inner = pick(stacked, upto)
        whole = pick(stacked, same)
        gains = []
        for i in range(2):
            for leaf in range(LEAVES):
                left, total = [], []
                for s in range(STATS):
                    at = ((i * LEAVES + leaf) * STATS + s) * FOLD
                    run = whole[at : at + FOLD]
                    for step in (1, 2, 4):
                        run = run + jnp.where(row >= step, pltpu.roll(run, step, 0), 0.0)
                    lower = jnp.where(row >= 1, pltpu.roll(run, 1, 0), 0.0)
                    left.append(inner[at : at + FOLD] + lower)
                    total.append(jnp.broadcast_to(run[FOLD - 1 : FOLD], (FOLD, WIDTH)))
                right = [t - a for t, a in zip(total, left)]
                raw = 0.5 * (
                    left[0] * left[0] / (left[1] + RIDGE)
                    + right[0] * right[0] / (right[1] + RIDGE)
                    - total[0] * total[0] / (total[1] + RIDGE)
                )
                value = jnp.where((left[2] >= MIN_CHILD) & (right[2] >= MIN_CHILD), raw, 0.0)
                gains.append(value)
                tops[leaf] = jnp.maximum(tops[leaf], value)
        z = pick(jnp.concatenate(gains, 0), order)
        for i in range(2):
            for leaf in range(LEAVES):
                at = (i * LEAVES + leaf) * FOLD
                piece = z[at : at + FOLD]
                out = jnp.where(apart == 0, piece, 0.0)
                for d in range(1, FOLD):
                    part = jnp.where(apart == d, piece, 0.0)
                    out = out + pltpu.roll(pltpu.roll(part, FOLD - d, 0), LOW * d, 1)
                gain_ref[leaf, c * PAIR + i * FOLD : c * PAIR + (i + 1) * FOLD, :] = out
    tops = [jnp.max(top, axis=(0, 1), keepdims=True) for top in tops]
    at = lax.broadcasted_iota(jnp.int32, top_ref.shape, 1)
    top = jnp.where(at == 0, tops[0], tops[1])
    top_ref[...] = top if before is None else jnp.maximum(top, before[...])


def gain(own, others, first, features, devices, done):
    count = len(own)
    top = (devices, 128)
    rows = count * PAIR
    return pl.pallas_call(
        functools.partial(gain_kernel, count),
        grid=(1,),
        in_specs=[pl.BlockSpec((1,) + SUMS, lambda i: (0,) * 6)] * (2 * count)
        + ([pl.BlockSpec(memory_space=pl.ANY), pl.BlockSpec(top, lambda i: (0, 0))] if done else []),
        out_specs=[
            pl.BlockSpec((LEAVES, rows, BINS), lambda i: (0, first // count, 0)),
            pl.BlockSpec(top, lambda i: (0, 0)),
        ],
        out_shape=[jax.ShapeDtypeStruct((LEAVES, features, BINS), F32), jax.ShapeDtypeStruct(top, F32)],
        input_output_aliases={2 * count: 0, 2 * count + 1: 1} if done else {},
        compiler_params=pltpu.CompilerParams(vmem_limit_bytes=VMEM_BYTES),
        cost_estimate=pl.CostEstimate(flops=1 << 30, bytes_accessed=1 << 20, transcendentals=0),
    )(*own, *others, *done)


def in_halves(ways, bits):
    if not bits:
        return ways
    return in_halves([w for w in ways if not w & bits[0]], bits[1:]) + in_halves(
        [w for w in ways if w & bits[0]], bits[1:]
    )


def joined(arrays):
    return arrays[0] if len(arrays) == 1 else jnp.concatenate(arrays, 0)


def in_turn(packed, done):
    return (*packed[:2], lax.optimization_barrier((packed[2], *done))[0])


def local(owners, devices, bin_codes, gradient, hessian, leaf_of_block, block_rows):
    row_total, feat_local = bin_codes.shape
    pos = lax.axis_index("rows").astype(jnp.int32)[None]
    room = -(-(row_total + 2 * TILE + BLOCK) // SPAN) * SPAN
    pairs = feat_local // owners // PAIR
    bits = [1 << b for b in range(owners.bit_length() - 1)]
    plan, orders = PLAN, ORDERS
    if (owners, pairs) != (8, 4):
        plan = [([(pair, side)], []) for pair in range(pairs) for side in (1, 0)]
        plan += [([], [pair for pair in range(pairs) for _ in bits[1:]])]
        orders = [bits] * pairs

    def ways_of(pair, side):
        first, *rest = orders[pair]
        kept = in_halves([w for w in range(owners) if not w & first], rest)
        kept = [w ^ first for w in kept] if side else kept
        return [kept[i : i + WAYS] for i in range(0, len(kept), WAYS)]

    def swap(x, bit):
        return lax.ppermute(x, "rows", [(i, i ^ bit) for i in range(owners)])

    first_rows = rows_of(feat_local // owners, [(0, ways_of(0, 1)[0])])
    *packed, first, info = pack(
        pos, leaf_of_block, block_rows, bin_codes, gradient, hessian, room, first_rows
    )
    packed = (*packed, info)
    keep, other = {}, {0: [swap(first, orders[0][0])]}
    left = {pair: orders[pair][1:] for pair in range(pairs)}
    for jobs, exchanges in plan:
        for n in range(owners // 2 // WAYS):
            todo = [job for job in jobs if n or job != (0, 1)]
            if not todo:
                continue
            sums = histogram(packed, owners, [(pair, ways_of(pair, side)[n]) for pair, side in todo])
            for (pair, side), x in zip(todo, sums):
                (other if side else keep).setdefault(pair, []).append(swap(x, orders[pair][0]) if side else x)
            packed = in_turn(packed, sums)
        moved = []
        for pair in exchanges:
            if isinstance(keep[pair], list):
                keep[pair], other[pair] = joined(keep[pair]), joined(other[pair])
            mine, theirs, (bit, *left[pair]) = keep[pair], other[pair], left[pair]
            half = mine.shape[0] // 2
            on = mine[half:] + theirs[half:]
            moved.append(on)
            keep[pair], other[pair] = mine[:half] + theirs[:half], swap(on, bit)
        packed = in_turn(packed, moved)
    done = ()
    for group in (range(pairs - 1), range(pairs - 1, pairs)):
        if group:
            done = gain(
                [keep[p] for p in group], [other[p] for p in group], group[0], feat_local // owners, devices, done
            )
    split_gain, best = done
    best = lax.all_to_all(best, ("rows", "feat"), 0, 0, tiled=True)
    return split_gain, jnp.max(best, axis=0)[:LEAVES]


def solution(mesh):
    return jax.shard_map(
        functools.partial(local, mesh.shape["rows"], mesh.size),
        mesh=mesh,
        in_specs=(P("rows", "feat"), P("rows"), P("rows"), P("rows"), P("rows")),
        out_specs=(P(None, ("feat", "rows"), None), P()),
        check_vma=False,
    )
```

```python
import functools

import jax
import jax.numpy as jnp
from jax import lax
from jax.experimental import pallas as pl
from jax.experimental.pallas import tpu as pltpu
from jax.sharding import PartitionSpec as P

BINS = 256
LEAVES = 2
BLOCK = 128
MIN_CHILD = 20
RIDGE = 1.0

STATS = 3
HIGH = 8
LOW = 32
FOLD = 8
PAIR = 2 * FOLD
WIDTH = LOW * FOLD
ROWS = HIGH * FOLD
DEPTH = STATS * ROWS
TILE = 256
BIG = 3 * TILE
SPAN = 512
WAYS = 4
ORDERS = ((2, 4, 1), (1, 2, 4), (1, 2, 4), (1, 2, 4))
PLAN = (
    ([(1, 1), (2, 1)], []),
    ([(0, 0), (1, 0)], [0, 1]),
    ([(3, 1), (2, 0)], [1, 2, 0]),
    ([(3, 0)], [2, 3]),
    ([], [3]),
)
SUMS = (2, LEAVES, STATS, FOLD, WIDTH)

BF = jnp.bfloat16
F32 = jnp.float32
VMEM_BYTES = 24 << 20
MOST_VMEM = 54 << 20


def nt(a, b):
    return lax.dot_general(a, b, (((1,), (1,)), ((), ())), preferred_element_type=F32)


def in_vmem(x):
    return pltpu.with_memory_space_constraint(x, pltpu.VMEM)


def live_up(count):
    return (count + 15) // 16 * 16


def tiles_of(total):
    return (total + TILE - 1) // TILE


def pack_kernel(
    blocks, first_rows,
    pos_ref, leaf_ref, rows_ref, codes_ref, grad_ref, hess_ref,
    table_ref, weight_ref, sums_ref, info_ref,
    arrived, held, rows_held, pair_held, total, offset, ends, in_sem, pair_sem,
):
    steps = blocks * BLOCK // SPAN
    per_step = SPAN // BLOCK
    feats = held.shape[1]

    def fetch(i):
        return pltpu.make_async_copy(
            codes_ref.at[pl.ds(pl.multiple_of(i * SPAN, SPAN), SPAN), :], arrived.at[i], in_sem.at[i]
        )

    pairs = [
        pltpu.make_async_copy(ref, pair_held.at[i], pair_sem.at[i]) for i, ref in enumerate((grad_ref, hess_ref))
    ]
    for copy in pairs:
        copy.start()
    for i in range(steps):
        fetch(i).start()

    def count(k, room):
        size, leaf = live_up(rows_ref[k]), leaf_ref[k]
        return room[0] + size * (1 - leaf), room[1] + size * leaf

    first, second = lax.fori_loop(0, blocks, count, (0, 0), unroll=4)
    start = tiles_of(first) * TILE + BLOCK

    def place(k, room):
        offset[k] = jnp.where(leaf_ref[k] == 0, room[0], room[1])
        room = count(k, room)
        ends[0, k], ends[1, k] = room
        return room

    lax.fori_loop(0, blocks, place, (0, start), unroll=4)
    info_ref[0] = tiles_of(first)
    info_ref[1] = tiles_of(second)
    info_ref[2] = start
    info_ref[3] = pos_ref[0]

    rows_held[...] = jnp.zeros_like(rows_held)
    for copy in pairs:
        copy.wait()
    grads, hessians = pair_held[0].astype(F32), pair_held[1].astype(F32)
    lane = lax.broadcasted_iota(jnp.int32, (8, BLOCK), 1)
    row = lax.broadcasted_iota(jnp.int32, (8, BLOCK), 0)
    rolled = []
    for k in range(blocks):
        grad = jnp.broadcast_to(grads[k : k + 1], (8, BLOCK))
        hess = jnp.broadcast_to(hessians[k : k + 1], (8, BLOCK))
        value = jnp.where(row == 0, grad, jnp.where(row == 1, hess, jnp.where(row == 2, 1.0, 0.0)))
        value = jnp.where(lane < rows_ref[k], value, 0.0)
        rolled.append(pltpu.roll(value, lax.rem(offset[k], BLOCK), 1))
    for k in range(blocks):
        at = offset[k]
        shift = lax.rem(at, BLOCK)
        tile = pl.multiple_of(at - shift, BLOCK)
        here = rows_held[:, pl.ds(tile, BLOCK)]
        rows_held[:, pl.ds(tile, BLOCK)] = jnp.where(lane < shift, here, rolled[k])
        after = pl.ds(pl.multiple_of(tile + BLOCK, BLOCK), BLOCK)
        rows_held[:, after] = jnp.where(lane < shift, rolled[k], 0.0)

    size = 256
    eye = (
        lax.broadcasted_iota(jnp.int32, (size, size), 0) == lax.broadcasted_iota(jnp.int32, (size, size), 1)
    ).astype(F32).astype(BF)

    def turn(base, tiles, done):
        @pl.loop(done, tiles)
        def _(j):
            at = pl.multiple_of(base + j * TILE, BLOCK)
            for f in range(0, feats, size):
                table_ref[f : f + size, pl.ds(at, TILE)] = nt(eye, held[pl.ds(at, TILE), f : f + size]).astype(BF)
            for s in range(STATS):
                weight_ref[s, :, pl.ds(at, TILE)] = jnp.broadcast_to(
                    rows_held[s : s + 1, pl.ds(at, TILE)], (16, TILE)
                ).astype(BF)

        return jnp.maximum(done, tiles)

    def step(i, done):
        fetch(i).wait()
        for j in range(per_step):
            at = pl.multiple_of(offset[i * per_step + j], 16)
            held[pl.ds(at, BLOCK), :] = arrived[i, j * BLOCK : (j + 1) * BLOCK, :].astype(F32).astype(BF)
        last = (i + 1) * per_step - 1
        return (
            turn(0, ends[0, last] // TILE, done[0]),
            turn(start, (ends[1, last] - start) // TILE, done[1]),
        )

    done = lax.fori_loop(0, steps, step, (0, 0))
    turn(0, tiles_of(first), done[0])
    turn(start, tiles_of(second), done[1])
    histogram_into(first_rows(info_ref), info_ref, table_ref, weight_ref, [sums_ref], total)


def pack(pos, leaf_of_block, block_rows, codes, gradient, hessian, room, first_rows):
    row_total, feat_local = codes.shape
    blocks = row_total // BLOCK
    steps = row_total // SPAN
    whole, anywhere = pl.BlockSpec(memory_space=pltpu.VMEM), pl.BlockSpec(memory_space=pl.ANY)
    return pl.pallas_call(
        functools.partial(pack_kernel, blocks, first_rows),
        grid_spec=pltpu.PrefetchScalarGridSpec(
            num_scalar_prefetch=3,
            grid=(1,),
            in_specs=[anywhere] * 3,
            out_specs=[whole, whole, whole, pl.BlockSpec(memory_space=pltpu.SMEM)],
            scratch_shapes=[
                pltpu.VMEM((steps, SPAN, feat_local), jnp.int32),
                pltpu.VMEM((room, feat_local), BF),
                pltpu.VMEM((8, room), F32),
                pltpu.VMEM((2, blocks, BLOCK), BF),
                pltpu.VMEM((2 * WAYS, DEPTH, WIDTH), F32),
                pltpu.SMEM((blocks,), jnp.int32),
                pltpu.SMEM((2, blocks), jnp.int32),
                pltpu.SemaphoreType.DMA((steps,)),
                pltpu.SemaphoreType.DMA((2,)),
            ],
        ),
        out_shape=[
            pltpu.VMEM((feat_local, room), BF),
            pltpu.VMEM((STATS, 16, room), BF),
            pltpu.VMEM((WAYS,) + SUMS, F32),
            pltpu.SMEM((8,), jnp.int32),
        ],
        compiler_params=pltpu.CompilerParams(vmem_limit_bytes=MOST_VMEM),
        cost_estimate=pl.CostEstimate(flops=4 << 30, bytes_accessed=16 << 20, transcendentals=0),
    )(pos, leaf_of_block, block_rows, codes, gradient.reshape(blocks, BLOCK), hessian.reshape(blocks, BLOCK))


def histogram_kernel(first_rows, info_ref, table_ref, weight_ref, *refs):
    histogram_into(first_rows(info_ref), info_ref, table_ref, weight_ref, refs[:-1], refs[-1])


def histogram_into(starts, info_ref, table_ref, weight_ref, outs, total):
    lane = lax.broadcasted_iota(jnp.int32, (FOLD, WIDTH), 1)
    skew = (lax.broadcasted_iota(jnp.int32, (FOLD, WIDTH), 0) - lane) & (FOLD - 1)

    def product(at, size, fresh):
        half = (lax.broadcasted_iota(jnp.int32, (16, size), 0) >> 3).astype(F32).astype(BF)
        nth = (lax.broadcasted_iota(jnp.int32, (size, 128), 1) >> 3).astype(F32).astype(BF)
        one, zero = jnp.ones((size, 128), BF), jnp.zeros((size, 128), BF)
        none = jnp.zeros((16, size), BF)
        weights = [weight_ref[s, :, pl.ds(at, size)] for s in range(STATS)]
        for way in range(len(starts)):
            both = table_ref[pl.ds(starts[way], PAIR), pl.ds(at, size)].astype(F32)
            for i in range(2):
                code = both[i * FOLD : (i + 1) * FOLD]
                high = jnp.floor(code * (1.0 / LOW))
                low = code - high * LOW
                high = jnp.concatenate([high] * 2, 0).astype(BF) - half
                masks = [high == BF(q) for q in range(0, HIGH, 2)]
                terms = jnp.concatenate([jnp.where(m, w, none) for w in weights for m in masks], 0)
                low = jnp.concatenate([jnp.concatenate([low] * 2, 0).astype(BF)] * 8, 0).T - nth
                picks = jnp.concatenate([jnp.where(low == BF(q), one, zero) for q in (0, 16)], 1)
                sums = lax.dot_general(terms, picks, (((1,), (0,)), ((), ())), preferred_element_type=F32)
                total[2 * way + i] = jnp.where(fresh, 0.0, total[2 * way + i]) + sums

    for leaf in range(LEAVES):
        start = info_ref[2] if leaf else 0
        tiles = info_ref[leaf]
        big = tiles // 3
        rest = tiles - 3 * big

        @pl.when(tiles == 0)
        def _():
            total[...] = jnp.zeros_like(total)

        @pl.loop(0, big)
        def _(k):
            product(pl.multiple_of(start + k * BIG, BLOCK), BIG, k == 0)

        at = start + big * BIG

        @pl.when(rest == 2)
        def _():
            product(pl.multiple_of(at, BLOCK), 2 * TILE, tiles == 2)

        @pl.when(rest == 1)
        def _():
            product(pl.multiple_of(at, BLOCK), TILE, tiles == 1)

        for way in range(len(starts)):
            for i in range(2):
                for s in range(STATS):
                    base = s * ROWS
                    value = total[2 * way + i, base : base + FOLD]
                    for h in range(1, HIGH):
                        piece = total[2 * way + i, base + h * FOLD : base + (h + 1) * FOLD]
                        value = jnp.where(skew == h, pltpu.roll(piece, h, 0), value)
                    outs[way // WAYS][way % WAYS, i, leaf, s] = value


def rows_of(per_owner, jobs):
    def first_rows(info_ref):
        return [
            pl.multiple_of((info_ref[3] ^ way) * per_owner + pair * PAIR, PAIR) for pair, ways in jobs for way in ways
        ]

    return first_rows


def histogram(packed, owners, jobs):
    table, weight, info = packed
    first_rows = rows_of(table.shape[0] // owners, jobs)
    whole = pl.BlockSpec(memory_space=pltpu.VMEM)
    return pl.pallas_call(
        functools.partial(histogram_kernel, first_rows),
        grid_spec=pltpu.PrefetchScalarGridSpec(
            num_scalar_prefetch=1,
            grid=(1,),
            in_specs=[whole, whole],
            out_specs=[whole] * len(jobs),
            scratch_shapes=[pltpu.VMEM((2 * WAYS * len(jobs), DEPTH, WIDTH), F32)],
        ),
        out_shape=[pltpu.VMEM((WAYS,) + SUMS, F32)] * len(jobs),
        compiler_params=pltpu.CompilerParams(vmem_limit_bytes=VMEM_BYTES),
        cost_estimate=pl.CostEstimate(flops=(6 << 30) * len(jobs), bytes_accessed=4 << 20, transcendentals=0),
    )(pltpu.with_memory_space_constraint(info, pltpu.SMEM), in_vmem(table), in_vmem(weight))


def pick(x, chooser):
    total = 0.0
    for _ in range(3):
        part = x.astype(BF)
        total = total + lax.dot_general(part, chooser, (((1,), (0,)), ((), ())), preferred_element_type=F32)
        x = x - part.astype(F32)
    return total


def gain_kernel(chunks, *refs):
    own, others, gain_ref, top_ref = refs[:chunks], refs[chunks : 2 * chunks], refs[-2], refs[-1]
    before = refs[2 * chunks + 1] if len(refs) > 2 * chunks + 2 else None
    lane = lax.broadcasted_iota(jnp.int32, (FOLD, WIDTH), 1)
    row = lax.broadcasted_iota(jnp.int32, (FOLD, WIDTH), 0)
    rows = lax.broadcasted_iota(jnp.int32, (WIDTH, WIDTH), 0)
    cols = lax.broadcasted_iota(jnp.int32, (WIDTH, WIDTH), 1)

    def chooser(mask):
        return jnp.where(mask, 1.0, 0.0).astype(BF)

    same = (rows & 7) == (cols & 7)
    upto = chooser(same & ((rows >> 3) <= (cols >> 3)))
    same = chooser(same)
    order = chooser(((rows & 7) == (cols >> 5)) & ((rows >> 3) == (cols & 31)))
    apart = (row - (lane >> 5)) & 7
    tops = [jnp.full((FOLD, WIDTH), -jnp.inf, F32)] * LEAVES
    for c in range(chunks):
        pieces = []
        for i in range(2):
            for leaf in range(LEAVES):
                for s in range(STATS):
                    x = own[c][0, i, leaf, s] + others[c][0, i, leaf, s]
                    for bit in (1, 2, 4):
                        x = jnp.where((lane & bit) != 0, pltpu.roll(x, FOLD - bit, 0), x)
                    pieces.append(x)
        stacked = jnp.concatenate(pieces, 0)
        inner = pick(stacked, upto)
        whole = pick(stacked, same)
        gains = []
        for i in range(2):
            for leaf in range(LEAVES):
                left, total = [], []
                for s in range(STATS):
                    at = ((i * LEAVES + leaf) * STATS + s) * FOLD
                    run = whole[at : at + FOLD]
                    for step in (1, 2, 4):
                        run = run + jnp.where(row >= step, pltpu.roll(run, step, 0), 0.0)
                    lower = jnp.where(row >= 1, pltpu.roll(run, 1, 0), 0.0)
                    left.append(inner[at : at + FOLD] + lower)
                    total.append(jnp.broadcast_to(run[FOLD - 1 : FOLD], (FOLD, WIDTH)))
                right = [t - a for t, a in zip(total, left)]
                raw = 0.5 * (
                    left[0] * left[0] / (left[1] + RIDGE)
                    + right[0] * right[0] / (right[1] + RIDGE)
                    - total[0] * total[0] / (total[1] + RIDGE)
                )
                value = jnp.where((left[2] >= MIN_CHILD) & (right[2] >= MIN_CHILD), raw, 0.0)
                gains.append(value)
                tops[leaf] = jnp.maximum(tops[leaf], value)
        z = pick(jnp.concatenate(gains, 0), order)
        for i in range(2):
            for leaf in range(LEAVES):
                at = (i * LEAVES + leaf) * FOLD
                piece = z[at : at + FOLD]
                out = jnp.where(apart == 0, piece, 0.0)
                for d in range(1, FOLD):
                    part = jnp.where(apart == d, piece, 0.0)
                    out = out + pltpu.roll(pltpu.roll(part, FOLD - d, 0), LOW * d, 1)
                gain_ref[leaf, c * PAIR + i * FOLD : c * PAIR + (i + 1) * FOLD, :] = out
    tops = [jnp.max(top, axis=(0, 1), keepdims=True) for top in tops]
    at = lax.broadcasted_iota(jnp.int32, top_ref.shape, 1)
    top = jnp.where(at == 0, tops[0], tops[1])
    top_ref[...] = top if before is None else jnp.maximum(top, before[...])


def gain(own, others, first, features, devices, done):
    count = len(own)
    top = (devices, 128)
    rows = count * PAIR
    return pl.pallas_call(
        functools.partial(gain_kernel, count),
        grid=(1,),
        in_specs=[pl.BlockSpec((1,) + SUMS, lambda i: (0,) * 6)] * (2 * count)
        + ([pl.BlockSpec(memory_space=pl.ANY), pl.BlockSpec(top, lambda i: (0, 0))] if done else []),
        out_specs=[
            pl.BlockSpec((LEAVES, rows, BINS), lambda i: (0, first // count, 0)),
            pl.BlockSpec(top, lambda i: (0, 0)),
        ],
        out_shape=[jax.ShapeDtypeStruct((LEAVES, features, BINS), F32), jax.ShapeDtypeStruct(top, F32)],
        input_output_aliases={2 * count: 0, 2 * count + 1: 1} if done else {},
        compiler_params=pltpu.CompilerParams(vmem_limit_bytes=VMEM_BYTES),
        cost_estimate=pl.CostEstimate(flops=1 << 30, bytes_accessed=1 << 20, transcendentals=0),
    )(*own, *others, *done)


def in_halves(ways, bits):
    if not bits:
        return ways
    return in_halves([w for w in ways if not w & bits[0]], bits[1:]) + in_halves(
        [w for w in ways if w & bits[0]], bits[1:]
    )


def joined(arrays):
    return arrays[0] if len(arrays) == 1 else jnp.concatenate(arrays, 0)


def in_turn(packed, done):
    return (*packed[:2], lax.optimization_barrier((packed[2], *done))[0])


def local(owners, devices, bin_codes, gradient, hessian, leaf_of_block, block_rows):
    row_total, feat_local = bin_codes.shape
    pos = lax.axis_index("rows").astype(jnp.int32)[None]
    room = -(-(row_total + 2 * TILE + BLOCK) // SPAN) * SPAN
    pairs = feat_local // owners // PAIR
    bits = [1 << b for b in range(owners.bit_length() - 1)]
    plan, orders = PLAN, ORDERS
    if (owners, pairs) != (8, 4):
        plan = [([(pair, side)], []) for pair in range(pairs) for side in (1, 0)]
        plan += [([], [pair for pair in range(pairs) for _ in bits[1:]])]
        orders = [bits] * pairs

    def ways_of(pair, side):
        first, *rest = orders[pair]
        kept = in_halves([w for w in range(owners) if not w & first], rest)
        kept = [w ^ first for w in kept] if side else kept
        return [kept[i : i + WAYS] for i in range(0, len(kept), WAYS)]

    def swap(x, bit):
        return lax.ppermute(x, "rows", [(i, i ^ bit) for i in range(owners)])

    first_rows = rows_of(feat_local // owners, [(0, ways_of(0, 1)[0])])
    *packed, first, info = pack(
        pos, leaf_of_block, block_rows, bin_codes, gradient, hessian, room, first_rows
    )
    packed = (*packed, info)
    keep, other = {}, {0: [swap(first, orders[0][0])]}
    left = {pair: orders[pair][1:] for pair in range(pairs)}
    early, done = range(pairs // 2), ()

    def gain_of(group):
        return gain([keep[p] for p in group], [other[p] for p in group], group[0], feat_local // owners, devices, done)

    for jobs, exchanges in plan:
        if early and not (done or jobs or any(left[pair] for pair in early)):
            done = gain_of(early)
            packed = in_turn(packed, done[1:])
        for n in range(owners // 2 // WAYS):
            todo = [job for job in jobs if n or job != (0, 1)]
            if not todo:
                continue
            sums = histogram(packed, owners, [(pair, ways_of(pair, side)[n]) for pair, side in todo])
            for (pair, side), x in zip(todo, sums):
                (other if side else keep).setdefault(pair, []).append(swap(x, orders[pair][0]) if side else x)
            packed = in_turn(packed, sums)
        moved = []
        for pair in exchanges:
            if isinstance(keep[pair], list):
                keep[pair], other[pair] = joined(keep[pair]), joined(other[pair])
            mine, theirs, (bit, *left[pair]) = keep[pair], other[pair], left[pair]
            half = mine.shape[0] // 2
            on = mine[half:] + theirs[half:]
            moved.append(on)
            keep[pair], other[pair] = mine[:half] + theirs[:half], swap(on, bit)
        packed = in_turn(packed, moved)
    if early and not done:
        done = gain_of(early)
    split_gain, best = gain_of(range(pairs // 2, pairs))
    best = lax.all_to_all(best, ("rows", "feat"), 0, 0, tiled=True)
    return split_gain, jnp.max(best, axis=0)[:LEAVES]


def solution(mesh):
    return jax.shard_map(
        functools.partial(local, mesh.shape["rows"], mesh.size),
        mesh=mesh,
        in_specs=(P("rows", "feat"), P("rows"), P("rows"), P("rows"), P("rows")),
        out_specs=(P(None, ("feat", "rows"), None), P()),
        check_vma=False,
    )
```
